32 devices in a mesh: shard: 2 (over y), ctx: 8 (over z, x), tp: 2 (over core).
Axes of the slice: x: 2, y: 2, z: 4, core: 2. Of those that a mesh axis runs over, the one named last changes fastest.
Arguments:
- tokens: bfloat16 [8192, 1024], P(('shard', 'ctx')), may hold values from -6 to 6
- cotangent: bfloat16 [8192, 1024], P(('shard', 'ctx')), may hold values from -6 to 6
- lengths: int32 [2, 4], P('shard'), may hold values from 1 to 4093, as said below
- g_attn: bfloat16 [1024], P('shard'), may hold values from 0.099609375 to 1.8984375
- w_qkv: bfloat16 [1024, 3, 1024], P('shard', None, 'tp'), may hold values from -0.1875 to 0.1875
- w_attn_out: bfloat16 [1024, 1024], P('tp', 'shard'), may hold values from -6 to 6
- g_mlp: bfloat16 [1024], P('shard'), may hold values from 0.099609375 to 1.8984375
- w_in: bfloat16 [1024, 2, 2624], P('shard', None, 'tp'), may hold values from -0.1875 to 0.1875
- w_mlp_out: bfloat16 [2624, 1024], P('tp', 'shard'), may hold values from -0.125 to 0.125
Outputs:
- output: bfloat16 [8192, 1024], P(('shard', 'ctx'))
- grad_tokens: bfloat16 [8192, 1024], P(('shard', 'ctx'))
- grad_g_attn: float32 [1024], P('shard')
- grad_w_qkv: float32 [1024, 3, 1024], P('shard', None, 'tp')
- grad_w_attn_out: float32 [1024, 1024], P('tp', 'shard')
- grad_g_mlp: float32 [1024], P('shard')
- grad_w_in: float32 [1024, 2, 2624], P('shard', None, 'tp')
- grad_w_mlp_out: float32 [2624, 1024], P('tp', 'shard')
The draws below stay inside these ranges and needn't reach their ends.
Inputs may be any that keep to these rules, and one draw needn't show every extreme that they name: `lengths`: each row sums to 4096. In every group one sequence, at a place drawn anew, starts within the first 512 tokens and ends within the last 512; the longest sequence of all groups has 4093 tokens.
All inputs are finite; a program needn't handle non-finite values.
Results may differ from the reference program's by a relative error of at most 0.024.
Values may be sent and summed in bfloat16 or wider, within the bound.
A program may use at most 128 MiB of HBM per device.

```python
import math
import jax
import jax.numpy as jnp
from jax import lax

D = 1024
H = 16
HD = 64
FF = 2624
SEQS = 4
TOK_DEV = 512
GROUP = 4096
GROUPS = 2
TOKENS = 8192


def draw_lengths(key, part):
    key = jax.random.fold_in(key, 17)
    short_key, place_key, row_key = jax.random.split(key, 3)
    short_most = max(1, (TOK_DEV - 1) // (SEQS - 1))
    shorter = jax.random.randint(short_key, (GROUPS, SEQS), 1, short_most + 1, dtype=jnp.int32)
    tiny_row = jax.random.randint(row_key, (), 0, GROUPS, dtype=jnp.int32)
    shorter = jnp.where(jnp.arange(GROUPS, dtype=jnp.int32)[:, None] == tiny_row, 1, shorter)
    longest = jax.random.randint(place_key, (GROUPS, 1), 0, SEQS, dtype=jnp.int32)
    chosen = jnp.arange(SEQS, dtype=jnp.int32)[None, :] == longest
    others = jnp.sum(jnp.where(chosen, 0, shorter), axis=1, keepdims=True).astype(jnp.int32)
    return jnp.where(chosen, GROUP - others, shorter).astype(jnp.int32)


def levels(own_key, dims, cuts, smallest, high):
    gain = 1.0
    for axis_at, blocks in cuts:
        steps = jax.random.uniform(jax.random.fold_in(jax.random.fold_in(own_key, 6), axis_at), (blocks,), jnp.float32, smallest / len(cuts), high / len(cuts))
        gain = gain * jnp.repeat(jnp.exp(steps), dims[axis_at] // blocks).reshape((-1,) + (1,) * (len(dims) - 1 - axis_at))
    return gain


def noise(stream_key, extent, width, bound, shards=(), held_as=jnp.bfloat16):
    drawn = jax.random.normal(stream_key, extent, jnp.float32) * width
    if len(shards) > 0:
        drawn = levels(stream_key, extent, shards, -0.22, 0.18) * drawn
    return jnp.clip(drawn, min=-bound, max=bound).astype(held_as)


def setup_inputs(seed: int = 0) -> dict:
    key_list = jax.random.split(jax.random.key(seed), 10)
    return {
        "tokens": noise(key_list[0], (TOKENS, D), 1.0, 6.0, ((0, 16),)),
        "cotangent": noise(key_list[1], (TOKENS, D), 1.0, 6.0, ((0, 16),)),
        "lengths": draw_lengths(jax.random.fold_in(key_list[9], 71), 0),
        "g_attn": jnp.clip(1.0 + 0.18 * jax.random.normal(key_list[3], (D,), jnp.float32), 0.099609375, 1.8984375).astype(jnp.bfloat16),
        "w_qkv": noise(key_list[4], (D, 3, D), D ** -0.5, 0.1875, ((0, 2), (2, 2))),
        "w_attn_out": noise(key_list[5], (D, D), (max(1, 2 * D // GROUP)) ** -0.5, 6.0, ((0, 2), (1, 2))),
        "g_mlp": jnp.clip(1.0 + 0.18 * jax.random.normal(key_list[6], (D,), jnp.float32), 0.099609375, 1.8984375).astype(jnp.bfloat16),
        "w_in": noise(key_list[7], (D, 2, FF), D ** -0.5, 0.1875, ((0, 2), (2, 2))),
        "w_mlp_out": noise(key_list[8], (FF, D), FF ** -0.5, 0.125, ((0, 2), (1, 2))),
    }


EPSILON = 1e-05
ROPE_BASE = 160000.0
MASKED = -1e+30
EXACT = lax.Precision.HIGHEST

@jax.custom_vjp
def low(v):
    return lax.optimization_barrier(v.astype(jnp.bfloat16)).astype(jnp.float32)

@jax.custom_vjp
def low_back(v):
    return v

def low_keep(v):
    return (low(v), None)

def low_pass(kept, grad):
    return (grad,)

def back_keep(v):
    return (v, None)

def back_low(kept, grad):
    return (low(grad),)
low.defvjp(low_keep, low_pass)
low_back.defvjp(back_keep, back_low)

def layer_norm(values, norm_gain):
    average = lax.optimization_barrier(jnp.mean(values, axis=-1, keepdims=True))
    centred = values - average
    spread = lax.optimization_barrier(jnp.mean(centred * centred, axis=-1, keepdims=True))
    return centred * lax.rsqrt(spread + EPSILON) * norm_gain

def rotate(values, cos_table, sin_table):
    half_size = values.shape[-1] // 2
    front_half = values[..., :half_size]
    back_half = values[..., half_size:]
    cos_rows = cos_table[:, None, :]
    sin_rows = sin_table[:, None, :]
    return jnp.concatenate([front_half * cos_rows - back_half * sin_rows, back_half * cos_rows + front_half * sin_rows], axis=-1)

def rope_tables(places, head_size):
    half_size = head_size // 2
    powers = jnp.arange(half_size, dtype=jnp.float32) * (-2.0 * math.log(ROPE_BASE) / head_size)
    angles = places.astype(jnp.float32)[:, None] * jnp.exp(powers)[None, :]
    return (jnp.cos(angles), jnp.sin(angles))

def positions_of(seq_lengths, places):
    seq_count = seq_lengths.shape[0]
    seq_ends = jnp.cumsum(seq_lengths).astype(jnp.int32)
    seq_starts = (seq_ends - seq_lengths).astype(jnp.int32)
    segment = lax.optimization_barrier(jnp.sum((places[:, None] >= seq_ends[None, :]).astype(jnp.int32), axis=1)).astype(jnp.int32)
    chosen = segment[:, None] == jnp.arange(seq_count, dtype=jnp.int32)[None, :]
    seq_first = lax.optimization_barrier(jnp.sum(jnp.where(chosen, seq_starts[None, :], 0), axis=1)).astype(jnp.int32)
    return (segment, (places - seq_first).astype(jnp.int32))

def geglu(lifted):
    return jax.nn.gelu(lifted[:, 0], approximate=False) * lifted[:, 1]

def attend_rows(queries, seg_query, key_rows, values, seg_keys):
    scores = low_back(jnp.einsum('qhd,khd->hqk', queries, key_rows, precision=EXACT) * (1.0 / math.sqrt(HD)))
    same_seg = (seg_query[:, None] == seg_keys[None, :])[None]
    scores = jnp.where(same_seg, scores, MASKED)
    largest = lax.optimization_barrier(jnp.max(scores, axis=-1, keepdims=True))
    raised = jnp.exp(scores - largest)
    weights = low(raised / lax.optimization_barrier(jnp.sum(raised, axis=-1, keepdims=True)))
    return jnp.einsum('hqk,khd->qhd', weights, values, precision=EXACT)

def attend_group(packed):
    queries, key_rows, values, segment = packed
    block_rows = math.gcd(GROUP, 512)
    blocks = (queries.reshape(GROUP // block_rows, block_rows, H, HD), segment.reshape(GROUP // block_rows, block_rows))
    saved = jax.checkpoint(attend_rows)
    result = lax.map(lambda parts: saved(parts[0], parts[1], key_rows, values, segment), blocks)
    return result.reshape(GROUP, H, HD)

def grouped(array_in):
    return array_in.reshape(GROUPS, GROUP, H, HD)

def reference(tokens, cotangent, lengths, g_attn, w_qkv, w_attn_out, g_mlp, w_in, w_mlp_out):
    places = jnp.arange(GROUP, dtype=jnp.int32)
    segment, inside = jax.vmap(lambda seq_row: positions_of(seq_row, places))(lengths)
    cos_table, sin_table = rope_tables(inside.reshape(TOKENS), HD)

    def forward(residual, gain_one, qkv_weight, out_weight, gain_two, in_weight, down_weight):
        hidden_one = low(layer_norm(residual, gain_one))
        projected = low_back(jnp.einsum('td,dcn->tcn', hidden_one, qkv_weight, precision=EXACT))
        split_heads = projected.reshape(TOKENS, 3, H, HD)
        queries = low(rotate(split_heads[:, 0], cos_table, sin_table))
        key_rows = low(rotate(split_heads[:, 1], cos_table, sin_table))
        values = low(split_heads[:, 2])
        attended = lax.map(attend_group, (grouped(queries), grouped(key_rows), grouped(values), segment))
        attended = low_back(low(attended.reshape(TOKENS, D)))
        middle = residual + low_back(jnp.dot(attended, out_weight, precision=EXACT))
        hidden_two = low(layer_norm(middle, gain_two))
        lifted = low_back(jnp.einsum('td,dcf->tcf', hidden_two, in_weight, precision=EXACT))
        mixed_low = low(geglu(lifted))
        return middle + low_back(jnp.dot(mixed_low, down_weight, precision=EXACT))
    floats = tuple((array_in.astype(jnp.float32) for array_in in (tokens, g_attn, w_qkv, w_attn_out, g_mlp, w_in, w_mlp_out)))
    output, pullback = jax.vjp(forward, *floats)
    grads = pullback(cotangent.astype(jnp.float32))
    return (output.astype(jnp.bfloat16), grads[0].astype(jnp.bfloat16), grads[1], grads[2], grads[3], grads[4], grads[5], grads[6])
```

```python
import functools
import math

import jax
import jax.numpy as jnp
from jax import lax
from jax.experimental import pallas as pl
from jax.experimental.pallas import tpu as pltpu
from jax.sharding import PartitionSpec as P

HD = 64


EPSILON = 1e-05
ROPE_BASE = 160000.0
MASKED = -1e30


def shifted(block, axis, distance):
    devices = range(lax.axis_size(axis))
    route = [((i - distance) % len(devices), i) for i in devices]
    return lax.ppermute(block, axis, route)


def layer_norm(values, norm_gain):
    average = jnp.mean(values, axis=-1, keepdims=True)
    centred = values - average
    spread = jnp.mean(centred * centred, axis=-1, keepdims=True)
    return centred * lax.rsqrt(spread + EPSILON) * norm_gain


def rotate(values, cos_table, sin_table):
    half_size = values.shape[-1] // 2
    front_half = values[..., :half_size]
    back_half = values[..., half_size:]
    cos_rows = cos_table[:, None, :]
    sin_rows = sin_table[:, None, :]
    return jnp.concatenate(
        [
            front_half * cos_rows - back_half * sin_rows,
            back_half * cos_rows + front_half * sin_rows,
        ],
        axis=-1,
    )


def rope_tables(places, head_size):
    half_size = head_size // 2
    powers = jnp.arange(half_size, dtype=jnp.float32) * (-2.0 * math.log(ROPE_BASE) / head_size)
    angles = places.astype(jnp.float32)[:, None] * jnp.exp(powers)[None, :]
    return (jnp.cos(angles), jnp.sin(angles))


def positions_of(seq_lengths, places):
    seq_count = seq_lengths.shape[0]
    seq_ends = jnp.cumsum(seq_lengths)
    seq_starts = seq_ends - seq_lengths
    segment = jnp.sum((places[:, None] >= seq_ends[None, :]).astype(jnp.int32), axis=1)
    chosen = segment[:, None] == jnp.arange(seq_count, dtype=jnp.int32)[None, :]
    seq_first = jnp.sum(jnp.where(chosen, seq_starts[None, :], 0), axis=1)
    return (segment, places - seq_first)


def geglu(lifted):
    return jax.nn.gelu(lifted[:, 0], approximate=False) * lifted[:, 1]


def split_block(kv_block, head_count):
    key_count = kv_block.shape[1]
    return (
        kv_block[0].reshape(key_count, head_count, -1),
        kv_block[1].reshape(key_count, head_count, -1),
    )


def masked_scores(queries, key_rows, seg_query, seg_keys, scaling):
    scores = (
        jnp.einsum("qhd,khd->hqk", queries, key_rows, preferred_element_type=jnp.float32) * scaling
    )
    same_seg = (seg_query[:, None] == seg_keys[None, :])[None]
    return (jnp.where(same_seg, scores, MASKED), same_seg)


def forward_step(soft_state, kv_block, seg_keys, queries, seg_query, scaling):
    maxima, totals, running = soft_state
    key_rows, values = split_block(kv_block, queries.shape[1])
    scores, same_seg = masked_scores(queries, key_rows, seg_query, seg_keys, scaling)
    new_max = jnp.maximum(maxima, jnp.max(scores, axis=-1))
    weights = jnp.where(same_seg, jnp.exp(scores - new_max[..., None]), 0.0)
    factor = jnp.exp(maxima - new_max)
    totals = totals * factor + jnp.sum(weights, axis=-1)
    update = jnp.einsum(
        "hqk,khd->hqd", weights.astype(jnp.bfloat16), values, preferred_element_type=jnp.float32
    )
    return (new_max, totals, running * factor[..., None] + update)


def backward_step(kv_block, seg_keys, queries, seg_query, grad_heads, log_sums, row_delta, scaling):
    key_rows, values = split_block(kv_block, queries.shape[1])
    scores, same_seg = masked_scores(queries, key_rows, seg_query, seg_keys, scaling)
    weights = jnp.where(same_seg, jnp.exp(scores - log_sums[..., None]), 0.0)
    grad_weights = jnp.einsum(
        "qhd,khd->hqk", grad_heads, values, preferred_element_type=jnp.float32
    )
    grad_scores = (weights * (grad_weights - row_delta[..., None])).astype(jnp.bfloat16)
    grad_query = (
        jnp.einsum("hqk,khd->qhd", grad_scores, key_rows, preferred_element_type=jnp.float32)
        * scaling
    )
    grad_keys = (
        jnp.einsum("hqk,qhd->khd", grad_scores, queries, preferred_element_type=jnp.float32)
        * scaling
    )
    grad_values = jnp.einsum(
        "hqk,qhd->khd", weights.astype(jnp.bfloat16), grad_heads, preferred_element_type=jnp.float32
    )
    key_count = key_rows.shape[0]
    return (
        grad_query,
        jnp.stack([grad_keys.reshape(key_count, -1), grad_values.reshape(key_count, -1)]),
    )


def shards(tokens, cotangent, lengths, g_attn, w_qkv, w_attn_out, g_mlp, w_in, w_mlp_out):
    tok_rows = tokens.shape[0]
    ctx_size = lax.axis_size("ctx")
    ctx_place = lax.axis_index("ctx")
    seq_lengths = lengths[0]
    row_index = jnp.arange(tok_rows, dtype=jnp.int32)
    segment_local, inside = positions_of(seq_lengths, ctx_place * tok_rows + row_index)
    cos_table, sin_table = rope_tables(inside, HD)
    scaling = 1.0 / math.sqrt(HD)

    def segments_from(source):
        return positions_of(seq_lengths, source * tok_rows + row_index)[0]

    attn_gain, qkv_full, out_full = (
        lax.all_gather(g_attn, "shard", axis=0, tiled=True),
        lax.all_gather(w_qkv, "shard", axis=0, tiled=True),
        lax.all_gather(w_attn_out, "shard", axis=1, tiled=True),
    )
    residual = tokens.astype(jnp.float32)
    normed_one, norm_one_back = jax.vjp(layer_norm, residual, attn_gain.astype(jnp.float32))
    hidden_one = normed_one.astype(jnp.bfloat16)
    projected = jnp.einsum("td,dcn->tcn", hidden_one, qkv_full, preferred_element_type=jnp.float32)
    local_width = projected.shape[2]
    head_count = local_width // HD
    split_heads = projected.reshape(tok_rows, 3, head_count, HD)
    queries = rotate(split_heads[:, 0], cos_table, sin_table).astype(jnp.bfloat16)
    key_rows = rotate(split_heads[:, 1], cos_table, sin_table).astype(jnp.bfloat16)
    values = split_heads[:, 2].astype(jnp.bfloat16)
    key_vals = jnp.stack(
        [key_rows.reshape(tok_rows, local_width), values.reshape(tok_rows, local_width)]
    )

    def attend(soft_state, kv_block, source):
        return forward_step(
            soft_state, kv_block, segments_from(source), queries, segment_local, scaling
        )

    start_state = (
        jnp.full((head_count, tok_rows), MASKED, jnp.float32),
        jnp.zeros((head_count, tok_rows), jnp.float32),
        jnp.zeros((head_count, tok_rows, HD), jnp.float32),
    )
    first_state = attend(start_state, key_vals, ctx_place)

    def pass_forward(step_index, carry):
        moving, soft_state = carry
        moving = shifted(moving, "ctx", 1)
        source = (ctx_place - step_index) % ctx_size
        return (moving, attend(soft_state, moving, source))

    _, soft_state = lax.fori_loop(1, ctx_size, pass_forward, (key_vals, first_state))
    maxima, totals, running = soft_state
    attended = running / totals[..., None]
    log_sums = maxima + jnp.log(totals)
    attn_low = (
        jnp.transpose(attended, (1, 0, 2)).reshape(tok_rows, local_width).astype(jnp.bfloat16)
    )
    attn_part = jnp.dot(attn_low, out_full, preferred_element_type=jnp.float32)
    middle = residual + lax.psum(attn_part.astype(jnp.bfloat16), "tp").astype(jnp.float32)
    mlp_gain, in_full, down_full = (
        lax.all_gather(g_mlp, "shard", axis=0, tiled=True),
        lax.all_gather(w_in, "shard", axis=0, tiled=True),
        lax.all_gather(w_mlp_out, "shard", axis=1, tiled=True),
    )
    normed_two, norm_two_back = jax.vjp(layer_norm, middle, mlp_gain.astype(jnp.float32))
    hidden_two = normed_two.astype(jnp.bfloat16)
    lifted = jnp.einsum("td,dcf->tcf", hidden_two, in_full, preferred_element_type=jnp.float32)
    mixed_f, geglu_back = jax.vjp(geglu, lifted)
    mixed_low = mixed_f.astype(jnp.bfloat16)
    mlp_part = jnp.dot(mixed_low, down_full, preferred_element_type=jnp.float32)
    output = (middle + lax.psum(mlp_part.astype(jnp.bfloat16), "tp").astype(jnp.float32)).astype(
        jnp.bfloat16
    )
    grad_down = jnp.einsum("tf,td->fd", mixed_low, cotangent, preferred_element_type=jnp.float32)
    grad_mixed = jnp.einsum("td,fd->tf", cotangent, down_full, preferred_element_type=jnp.float32)
    (grad_lifted,) = geglu_back(grad_mixed)
    lifted_low = grad_lifted.astype(jnp.bfloat16)
    grad_in = jnp.einsum("td,tcf->dcf", hidden_two, lifted_low, preferred_element_type=jnp.float32)
    hidden_two_part = jnp.einsum(
        "tcf,dcf->td", lifted_low, in_full, preferred_element_type=jnp.float32
    )
    grad_hidden_two = lax.psum(hidden_two_part.astype(jnp.bfloat16), "tp").astype(jnp.float32)
    grad_middle_norm, grad_mlp_gain = norm_two_back(grad_hidden_two)
    grad_middle = cotangent.astype(jnp.float32) + grad_middle_norm
    grad_branch = grad_middle.astype(jnp.bfloat16)
    grad_attn_out = jnp.einsum(
        "tn,td->nd", attn_low, grad_branch, preferred_element_type=jnp.float32
    )
    grad_attended = jnp.einsum(
        "td,nd->tn", grad_branch, out_full, preferred_element_type=jnp.float32
    ).astype(jnp.bfloat16)
    grad_heads = grad_attended.reshape(tok_rows, head_count, HD)
    row_delta = jnp.sum(
        jnp.transpose(grad_heads.astype(jnp.float32), (1, 0, 2)) * attended, axis=-1
    )

    def back_block(kv_block, source):
        return backward_step(
            kv_block,
            segments_from(source),
            queries,
            segment_local,
            grad_heads,
            log_sums,
            row_delta,
            scaling,
        )

    grad_query, grad_block = back_block(key_vals, ctx_place)

    def pass_backward(step_index, carry):
        moving, carried, grad_sofar = carry
        moving = shifted(moving, "ctx", 1)
        carried = shifted(carried.astype(jnp.bfloat16), "ctx", 1).astype(carried.dtype)
        source = (ctx_place - step_index) % ctx_size
        more_query, more_block = back_block(moving, source)
        return (moving, carried + more_block, grad_sofar + more_query)

    _, carried, grad_query = lax.fori_loop(
        1, ctx_size, pass_backward, (key_vals, grad_block, grad_query)
    )
    grad_keyvals = shifted(carried.astype(jnp.bfloat16), "ctx", 1).astype(carried.dtype)
    grad_keys = grad_keyvals[0].reshape(tok_rows, head_count, HD)
    grad_values = grad_keyvals[1].reshape(tok_rows, head_count, HD)
    grad_projected = jnp.stack(
        [
            rotate(grad_query, cos_table, -sin_table),
            rotate(grad_keys, cos_table, -sin_table),
            grad_values,
        ],
        axis=1,
    )
    grad_projected = grad_projected.reshape(tok_rows, 3, local_width).astype(jnp.bfloat16)
    grad_qkv = jnp.einsum(
        "td,tcn->dcn", hidden_one, grad_projected, preferred_element_type=jnp.float32
    )
    hidden_one_part = jnp.einsum(
        "tcn,dcn->td", grad_projected, qkv_full, preferred_element_type=jnp.float32
    )
    grad_hidden_one = lax.psum(hidden_one_part.astype(jnp.bfloat16), "tp").astype(jnp.float32)
    grad_input_norm, grad_attn_gain = norm_one_back(grad_hidden_one)
    grad_tokens = (grad_middle + grad_input_norm).astype(jnp.bfloat16)
    sharded = (
        lax.psum_scatter(
            grad_attn_gain.astype(jnp.bfloat16), "shard", scatter_dimension=0, tiled=True
        ).astype(jnp.float32),
        lax.psum_scatter(
            grad_qkv.astype(jnp.bfloat16), "shard", scatter_dimension=0, tiled=True
        ).astype(jnp.float32),
        lax.psum_scatter(
            grad_attn_out.astype(jnp.bfloat16), "shard", scatter_dimension=1, tiled=True
        ).astype(jnp.float32),
        lax.psum_scatter(
            grad_mlp_gain.astype(jnp.bfloat16), "shard", scatter_dimension=0, tiled=True
        ).astype(jnp.float32),
        lax.psum_scatter(
            grad_in.astype(jnp.bfloat16), "shard", scatter_dimension=0, tiled=True
        ).astype(jnp.float32),
        lax.psum_scatter(
            grad_down.astype(jnp.bfloat16), "shard", scatter_dimension=1, tiled=True
        ).astype(jnp.float32),
    )
    summed = (
        lax.psum(sharded[0].astype(jnp.bfloat16), "ctx").astype(jnp.float32),
        lax.psum(sharded[1].astype(jnp.bfloat16), "ctx").astype(jnp.float32),
        lax.psum(sharded[2].astype(jnp.bfloat16), "ctx").astype(jnp.float32),
        lax.psum(sharded[3].astype(jnp.bfloat16), "ctx").astype(jnp.float32),
        lax.psum(sharded[4].astype(jnp.bfloat16), "ctx").astype(jnp.float32),
        lax.psum(sharded[5].astype(jnp.bfloat16), "ctx").astype(jnp.float32),
    )
    return (output, grad_tokens, summed[0], summed[1], summed[2], summed[3], summed[4], summed[5])


LOG2E = 1.4426950408889634
VMEM_BYTES = 56 * 1024 * 1024


def rope_tables_t(places, head_size):
    half_size = head_size // 2
    powers = jnp.arange(half_size, dtype=jnp.float32) * (-2.0 * math.log(ROPE_BASE) / head_size)
    angles = jnp.exp(powers)[:, None] * places.astype(jnp.float32)[None, :]
    return (jnp.cos(angles), jnp.sin(angles))


def rotate_t(values, cos_t, sin_t):
    half_size = values.shape[-2] // 2
    front, back = values[..., :half_size, :], values[..., half_size:, :]
    return jnp.concatenate(
        [front * cos_t - back * sin_t, back * cos_t + front * sin_t], axis=-2
    )


def segment_ids(ends_ref, positions):
    ids = jnp.zeros(positions.shape, jnp.int32)
    for i in range(ends_ref.shape[1]):
        ids += (positions >= ends_ref[0, i]).astype(jnp.int32)
    return ids


def forward_kernel(blocks, ends_ref, q_ref, k_ref, v_ref, low_ref, out_ref, lse_ref, v_rows):
    step = pl.program_id(1)
    size = q_ref.shape[3]

    @pl.when(step == 0)
    def _():
        lane = lax.broadcasted_iota(jnp.int32, (size, HD), 1)
        ones = jnp.where(lane == 0, 1.0, 0.0).astype(jnp.bfloat16)
        for j in range(blocks):
            v_rows[j, :, :HD] = v_ref[j, 0].T
            v_rows[j, :, HD:] = ones

    queries = q_ref[0, 0].T
    scale = LOG2E / math.sqrt(HD)

    def run(masked):
        rows_id = None
        scores = []
        top = None
        for j in range(blocks):
            part = jnp.dot(queries, k_ref[j, 0], preferred_element_type=jnp.float32)
            if masked or j in (0, blocks - 1):
                if rows_id is None:
                    rows_id = segment_ids(
                        ends_ref, step * size + lax.broadcasted_iota(jnp.int32, (size, 1), 0)
                    )
                keys_id = segment_ids(
                    ends_ref, j * size + lax.broadcasted_iota(jnp.int32, (1, size), 1)
                )
                part = jnp.where(rows_id == keys_id, part, MASKED)
            scores.append(part)
            most = jnp.max(part, axis=1, keepdims=True)
            top = most if top is None else jnp.maximum(top, most)
        offset = top * scale
        total = None
        for j in range(blocks):
            raised = jnp.exp2(scores[j] * scale - offset).astype(jnp.bfloat16)
            part = jnp.dot(raised, v_rows[j], preferred_element_type=jnp.float32)
            total = part if total is None else total + part
        flat = total.T
        sums = flat[HD : HD + 1]
        result = flat[:HD] / sums
        out_ref[0, 0] = result
        low_ref[0, 0] = result.astype(jnp.bfloat16)
        lse_ref[0, 0] = offset.T + jnp.log2(sums)

    edge = (step == 0) | (step == blocks - 1)
    pl.when(edge)(lambda: run(True))
    pl.when(jnp.logical_not(edge))(lambda: run(False))


def backward_kernel(
    blocks, ends_ref, q_ref, k_ref, v_ref, do_ref, o_ref, lse_ref, grad_ref, k_rows, v_rows, dk, dv
):
    step = pl.program_id(1)
    size = q_ref.shape[3]

    @pl.when(step == 0)
    def _():
        for j in range(blocks):
            k_rows[j] = k_ref[j, 0].T
            v_rows[j] = v_ref[j, 0].T
        dk[...] = jnp.zeros_like(dk)
        dv[...] = jnp.zeros_like(dv)

    scale = LOG2E / math.sqrt(HD)
    queries_t = q_ref[0, 0]
    queries = queries_t.T
    grads_t = do_ref[0, 0]
    grads = grads_t.T
    delta = jnp.sum(grads_t.astype(jnp.float32) * o_ref[0, 0], axis=0, keepdims=True)
    lse = lse_ref[0, 0]

    def run(masked):
        dq = jnp.zeros((size, HD), jnp.float32)
        queries_id = None
        for j in range(blocks):
            scores = jnp.dot(k_rows[j], queries_t, preferred_element_type=jnp.float32)
            weights = jnp.exp2(scores * scale - lse)
            if masked or j in (0, blocks - 1):
                if queries_id is None:
                    queries_id = segment_ids(
                        ends_ref, step * size + lax.broadcasted_iota(jnp.int32, (1, size), 1)
                    )
                keys_id = segment_ids(
                    ends_ref, j * size + lax.broadcasted_iota(jnp.int32, (size, 1), 0)
                )
                weights = jnp.where(queries_id == keys_id, weights, 0.0)
            grad_weights = jnp.dot(v_rows[j], grads_t, preferred_element_type=jnp.float32)
            grad_scores = (weights * (grad_weights - delta)).astype(jnp.bfloat16)
            dv[j] += jnp.dot(
                weights.astype(jnp.bfloat16), grads, preferred_element_type=jnp.float32
            )
            dk[j] += jnp.dot(grad_scores, queries, preferred_element_type=jnp.float32)
            dq += lax.dot_general(
                grad_scores, k_rows[j], (((0,), (0,)), ((), ())), preferred_element_type=jnp.float32
            )
        grad_ref[step, 0, :HD] = (dq * (1.0 / math.sqrt(HD))).T.astype(jnp.bfloat16)

    edge = (step == 0) | (step == blocks - 1)
    pl.when(edge)(lambda: run(True))
    pl.when(jnp.logical_not(edge))(lambda: run(False))

    @pl.when(step == blocks - 1)
    def _():
        for j in range(blocks):
            grad_ref[j, 0, HD : 2 * HD] = (dk[j] * (1.0 / math.sqrt(HD))).T.astype(jnp.bfloat16)
            grad_ref[j, 0, 2 * HD :] = dv[j].T.astype(jnp.bfloat16)


def packed_specs(blocks, size):
    return [
        pl.BlockSpec(memory_space=pltpu.SMEM),
        pl.BlockSpec((1, 1, HD, size), lambda h, i: (i, h, 0, 0)),
        pl.BlockSpec((blocks, 1, HD, size), lambda h, i: (0, h, 1, 0)),
        pl.BlockSpec((blocks, 1, HD, size), lambda h, i: (0, h, 2, 0)),
    ]


def attention_forward(ends, packed):
    blocks, heads, _, size = packed.shape
    pairs = heads * (blocks * size) ** 2
    tile = pl.BlockSpec((1, 1, HD, size), lambda h, i: (i, h, 0, 0))
    line = pl.BlockSpec((1, 1, 1, size), lambda h, i: (i, h, 0, 0))
    return pl.pallas_call(
        functools.partial(forward_kernel, blocks),
        grid=(heads, blocks),
        in_specs=packed_specs(blocks, size),
        out_specs=[tile, tile, line],
        out_shape=[
            jax.ShapeDtypeStruct((blocks, heads, HD, size), jnp.bfloat16),
            jax.ShapeDtypeStruct((blocks, heads, HD, size), jnp.float32),
            jax.ShapeDtypeStruct((blocks, heads, 1, size), jnp.float32),
        ],
        scratch_shapes=[pltpu.VMEM((blocks, size, 2 * HD), jnp.bfloat16)],
        compiler_params=pltpu.CompilerParams(vmem_limit_bytes=VMEM_BYTES),
        cost_estimate=pl.CostEstimate(
            flops=16 * HD * pairs, bytes_accessed=packed.size * 6, transcendentals=pairs
        ),
        name="attention_forward",
    )(ends, packed, packed, packed)


def attention_backward(ends, packed, grads, attended, lse):
    blocks, heads, _, size = packed.shape
    pairs = heads * (blocks * size) ** 2
    tile = pl.BlockSpec((1, 1, HD, size), lambda h, i: (i, h, 0, 0))
    line = pl.BlockSpec((1, 1, 1, size), lambda h, i: (i, h, 0, 0))
    return pl.pallas_call(
        functools.partial(backward_kernel, blocks),
        grid=(heads, blocks),
        in_specs=packed_specs(blocks, size) + [tile, tile, line],
        out_specs=pl.BlockSpec((blocks, 1, 3 * HD, size), lambda h, i: (0, h, 0, 0)),
        out_shape=jax.ShapeDtypeStruct(packed.shape, jnp.bfloat16),
        scratch_shapes=[
            pltpu.VMEM((blocks, size, HD), jnp.bfloat16),
            pltpu.VMEM((blocks, size, HD), jnp.bfloat16),
            pltpu.VMEM((blocks, size, HD), jnp.float32),
            pltpu.VMEM((blocks, size, HD), jnp.float32),
        ],
        compiler_params=pltpu.CompilerParams(vmem_limit_bytes=VMEM_BYTES),
        cost_estimate=pl.CostEstimate(
            flops=40 * HD * pairs, bytes_accessed=packed.size * 10, transcendentals=pairs
        ),
        name="attention_backward",
    )(ends, packed, packed, packed, grads, attended, lse)


def exchanged(array_in):
    return lax.all_to_all(array_in, "ctx", split_axis=0, concat_axis=0, tiled=True)


def head_shards(tokens, cotangent, lengths, g_attn, w_qkv, w_attn_out, g_mlp, w_in, w_mlp_out):
    tok_rows = tokens.shape[0]
    ctx_size = lax.axis_size("ctx")
    ctx_place = lax.axis_index("ctx")
    row_index = jnp.arange(tok_rows, dtype=jnp.int32)
    _, inside = positions_of(lengths[0], ctx_place * tok_rows + row_index)
    cos_t, sin_t = rope_tables_t(inside, HD)
    ends = jnp.cumsum(lengths, axis=1).astype(jnp.int32)

    attn_gain, qkv_full = (
        lax.all_gather(g_attn, "shard", axis=0, tiled=True),
        lax.all_gather(w_qkv, "shard", axis=0, tiled=True),
    )
    out_full = lax.all_gather(w_attn_out, "shard", axis=1, tiled=True)
    residual = tokens.astype(jnp.float32)
    normed_one, norm_one_back = jax.vjp(layer_norm, residual, attn_gain.astype(jnp.float32))
    hidden_one = normed_one.astype(jnp.bfloat16)
    projected = jnp.einsum("td,dcn->cnt", hidden_one, qkv_full, preferred_element_type=jnp.float32)
    local_width = projected.shape[1]
    head_count = local_width // HD
    own_heads = head_count // ctx_size
    split_heads = projected.reshape(3, head_count, HD, tok_rows)
    packed = jnp.concatenate(
        [
            rotate_t(split_heads[0], cos_t, sin_t).astype(jnp.bfloat16),
            rotate_t(split_heads[1], cos_t, sin_t).astype(jnp.bfloat16),
            split_heads[2].astype(jnp.bfloat16),
        ],
        axis=1,
    ).reshape(ctx_size, own_heads, 3 * HD, tok_rows)
    packed = exchanged(packed)
    own_low, own_attended, lse = attention_forward(ends, packed)
    attn_low = exchanged(own_low).reshape(local_width, tok_rows)
    attn_part = jnp.einsum("nt,nd->td", attn_low, out_full, preferred_element_type=jnp.float32)
    middle = residual + lax.psum(attn_part.astype(jnp.bfloat16), "tp").astype(jnp.float32)
    mlp_gain, in_full, down_full = (
        lax.all_gather(g_mlp, "shard", axis=0, tiled=True),
        lax.all_gather(w_in, "shard", axis=0, tiled=True),
        lax.all_gather(w_mlp_out, "shard", axis=1, tiled=True),
    )
    normed_two, norm_two_back = jax.vjp(layer_norm, middle, mlp_gain.astype(jnp.float32))
    hidden_two = normed_two.astype(jnp.bfloat16)
    lifted = jnp.einsum("td,dcf->tcf", hidden_two, in_full, preferred_element_type=jnp.float32)
    mixed_f, geglu_back = jax.vjp(geglu, lifted)
    mixed_low = mixed_f.astype(jnp.bfloat16)
    mlp_part = jnp.dot(mixed_low, down_full, preferred_element_type=jnp.float32)
    output = (middle + lax.psum(mlp_part.astype(jnp.bfloat16), "tp").astype(jnp.float32)).astype(
        jnp.bfloat16
    )
    grad_down = jnp.einsum("tf,td->fd", mixed_low, cotangent, preferred_element_type=jnp.float32)
    grad_mixed = jnp.einsum("td,fd->tf", cotangent, down_full, preferred_element_type=jnp.float32)
    (grad_lifted,) = geglu_back(grad_mixed)
    lifted_low = grad_lifted.astype(jnp.bfloat16)
    grad_in = jnp.einsum("td,tcf->dcf", hidden_two, lifted_low, preferred_element_type=jnp.float32)
    hidden_two_part = jnp.einsum(
        "tcf,dcf->td", lifted_low, in_full, preferred_element_type=jnp.float32
    )
    grad_hidden_two = lax.psum(hidden_two_part.astype(jnp.bfloat16), "tp").astype(jnp.float32)
    grad_middle_norm, grad_mlp_gain = norm_two_back(grad_hidden_two)
    grad_middle = cotangent.astype(jnp.float32) + grad_middle_norm
    grad_branch = grad_middle.astype(jnp.bfloat16)
    grad_attn_out = jnp.einsum(
        "nt,td->nd", attn_low, grad_branch, preferred_element_type=jnp.float32
    )
    grad_attended = jnp.einsum(
        "td,nd->nt", grad_branch, out_full, preferred_element_type=jnp.float32
    ).astype(jnp.bfloat16)
    own_grads = exchanged(grad_attended.reshape(ctx_size, own_heads, HD, tok_rows))
    own_packed = attention_backward(ends, packed, own_grads, own_attended, lse)
    grad_packed = exchanged(own_packed).reshape(head_count, 3, HD, tok_rows)
    grad_projected = jnp.stack(
        [
            rotate_t(grad_packed[:, 0].astype(jnp.float32), cos_t, -sin_t).astype(jnp.bfloat16),
            rotate_t(grad_packed[:, 1].astype(jnp.float32), cos_t, -sin_t).astype(jnp.bfloat16),
            grad_packed[:, 2],
        ],
        axis=0,
    ).reshape(3, local_width, tok_rows)
    grad_qkv = jnp.einsum(
        "td,cnt->dcn", hidden_one, grad_projected, preferred_element_type=jnp.float32
    )
    hidden_one_part = jnp.einsum(
        "cnt,dcn->td", grad_projected, qkv_full, preferred_element_type=jnp.float32
    )
    grad_hidden_one = lax.psum(hidden_one_part.astype(jnp.bfloat16), "tp").astype(jnp.float32)
    grad_input_norm, grad_attn_gain = norm_one_back(grad_hidden_one)
    grad_tokens = (grad_middle + grad_input_norm).astype(jnp.bfloat16)

    def owned(partial, dimension):
        part = lax.psum_scatter(
            partial.astype(jnp.bfloat16), "shard", scatter_dimension=dimension, tiled=True
        )
        return lax.psum(part, "ctx").astype(jnp.float32)

    return (
        output,
        grad_tokens,
        owned(grad_attn_gain, 0),
        owned(grad_qkv, 0),
        owned(grad_attn_out, 1),
        owned(grad_mlp_gain, 0),
        owned(grad_in, 0),
        owned(grad_down, 1),
    )


def layer(tokens, cotangent, lengths, g_attn, w_qkv, w_attn_out, g_mlp, w_in, w_mlp_out):
    head_count = w_qkv.shape[2] // HD
    whole_heads = head_count % lax.axis_size("ctx") == 0
    return (head_shards if whole_heads else shards)(
        tokens, cotangent, lengths, g_attn, w_qkv, w_attn_out, g_mlp, w_in, w_mlp_out
    )


def solution(mesh):
    return jax.shard_map(
        layer,
        mesh=mesh,
        in_specs=(
            P(("shard", "ctx"), None),
            P(("shard", "ctx"), None),
            P("shard", None),
            P("shard"),
            P("shard", None, "tp"),
            P("tp", "shard"),
            P("shard"),
            P("shard", None, "tp"),
            P("tp", "shard"),
        ),
        out_specs=(
            P(("shard", "ctx"), None),
            P(("shard", "ctx"), None),
            P("shard"),
            P("shard", None, "tp"),
            P("tp", "shard"),
            P("shard"),
            P("shard", None, "tp"),
            P("tp", "shard"),
        ),
        check_vma=False,
    )
```

```python
import functools
import math

import jax
import jax.numpy as jnp
from jax import lax
from jax.experimental import pallas as pl
from jax.experimental.pallas import tpu as pltpu
from jax.sharding import PartitionSpec as P

HD = 64


EPSILON = 1e-05
ROPE_BASE = 160000.0
MASKED = -1e30


def shifted(block, axis, distance):
    devices = range(lax.axis_size(axis))
    route = [((i - distance) % len(devices), i) for i in devices]
    return lax.ppermute(block, axis, route)


def layer_norm(values, norm_gain):
    average = jnp.mean(values, axis=-1, keepdims=True)
    centred = values - average
    spread = jnp.mean(centred * centred, axis=-1, keepdims=True)
    return centred * lax.rsqrt(spread + EPSILON) * norm_gain


def rotate(values, cos_table, sin_table):
    half_size = values.shape[-1] // 2
    front_half = values[..., :half_size]
    back_half = values[..., half_size:]
    cos_rows = cos_table[:, None, :]
    sin_rows = sin_table[:, None, :]
    return jnp.concatenate(
        [
            front_half * cos_rows - back_half * sin_rows,
            back_half * cos_rows + front_half * sin_rows,
        ],
        axis=-1,
    )


def rope_tables(places, head_size):
    half_size = head_size // 2
    powers = jnp.arange(half_size, dtype=jnp.float32) * (-2.0 * math.log(ROPE_BASE) / head_size)
    angles = places.astype(jnp.float32)[:, None] * jnp.exp(powers)[None, :]
    return (jnp.cos(angles), jnp.sin(angles))


def positions_of(seq_lengths, places):
    seq_count = seq_lengths.shape[0]
    seq_ends = jnp.cumsum(seq_lengths)
    seq_starts = seq_ends - seq_lengths
    segment = jnp.sum((places[:, None] >= seq_ends[None, :]).astype(jnp.int32), axis=1)
    chosen = segment[:, None] == jnp.arange(seq_count, dtype=jnp.int32)[None, :]
    seq_first = jnp.sum(jnp.where(chosen, seq_starts[None, :], 0), axis=1)
    return (segment, places - seq_first)


def geglu(lifted):
    return jax.nn.gelu(lifted[:, 0], approximate=False) * lifted[:, 1]


def split_block(kv_block, head_count):
    key_count = kv_block.shape[1]
    return (
        kv_block[0].reshape(key_count, head_count, -1),
        kv_block[1].reshape(key_count, head_count, -1),
    )


def masked_scores(queries, key_rows, seg_query, seg_keys, scaling):
    scores = (
        jnp.einsum("qhd,khd->hqk", queries, key_rows, preferred_element_type=jnp.float32) * scaling
    )
    same_seg = (seg_query[:, None] == seg_keys[None, :])[None]
    return (jnp.where(same_seg, scores, MASKED), same_seg)


def forward_step(soft_state, kv_block, seg_keys, queries, seg_query, scaling):
    maxima, totals, running = soft_state
    key_rows, values = split_block(kv_block, queries.shape[1])
    scores, same_seg = masked_scores(queries, key_rows, seg_query, seg_keys, scaling)
    new_max = jnp.maximum(maxima, jnp.max(scores, axis=-1))
    weights = jnp.where(same_seg, jnp.exp(scores - new_max[..., None]), 0.0)
    factor = jnp.exp(maxima - new_max)
    totals = totals * factor + jnp.sum(weights, axis=-1)
    update = jnp.einsum(
        "hqk,khd->hqd", weights.astype(jnp.bfloat16), values, preferred_element_type=jnp.float32
    )
    return (new_max, totals, running * factor[..., None] + update)


def backward_step(kv_block, seg_keys, queries, seg_query, grad_heads, log_sums, row_delta, scaling):
    key_rows, values = split_block(kv_block, queries.shape[1])
    scores, same_seg = masked_scores(queries, key_rows, seg_query, seg_keys, scaling)
    weights = jnp.where(same_seg, jnp.exp(scores - log_sums[..., None]), 0.0)
    grad_weights = jnp.einsum(
        "qhd,khd->hqk", grad_heads, values, preferred_element_type=jnp.float32
    )
    grad_scores = (weights * (grad_weights - row_delta[..., None])).astype(jnp.bfloat16)
    grad_query = (
        jnp.einsum("hqk,khd->qhd", grad_scores, key_rows, preferred_element_type=jnp.float32)
        * scaling
    )
    grad_keys = (
        jnp.einsum("hqk,qhd->khd", grad_scores, queries, preferred_element_type=jnp.float32)
        * scaling
    )
    grad_values = jnp.einsum(
        "hqk,qhd->khd", weights.astype(jnp.bfloat16), grad_heads, preferred_element_type=jnp.float32
    )
    key_count = key_rows.shape[0]
    return (
        grad_query,
        jnp.stack([grad_keys.reshape(key_count, -1), grad_values.reshape(key_count, -1)]),
    )


def shards(tokens, cotangent, lengths, g_attn, w_qkv, w_attn_out, g_mlp, w_in, w_mlp_out):
    tok_rows = tokens.shape[0]
    ctx_size = lax.axis_size("ctx")
    ctx_place = lax.axis_index("ctx")
    seq_lengths = lengths[0]
    row_index = jnp.arange(tok_rows, dtype=jnp.int32)
    segment_local, inside = positions_of(seq_lengths, ctx_place * tok_rows + row_index)
    cos_table, sin_table = rope_tables(inside, HD)
    scaling = 1.0 / math.sqrt(HD)

    def segments_from(source):
        return positions_of(seq_lengths, source * tok_rows + row_index)[0]

    attn_gain, qkv_full, out_full = (
        lax.all_gather(g_attn, "shard", axis=0, tiled=True),
        lax.all_gather(w_qkv, "shard", axis=0, tiled=True),
        lax.all_gather(w_attn_out, "shard", axis=1, tiled=True),
    )
    residual = tokens.astype(jnp.float32)
    normed_one, norm_one_back = jax.vjp(layer_norm, residual, attn_gain.astype(jnp.float32))
    hidden_one = normed_one.astype(jnp.bfloat16)
    projected = jnp.einsum("td,dcn->tcn", hidden_one, qkv_full, preferred_element_type=jnp.float32)
    local_width = projected.shape[2]
    head_count = local_width // HD
    split_heads = projected.reshape(tok_rows, 3, head_count, HD)
    queries = rotate(split_heads[:, 0], cos_table, sin_table).astype(jnp.bfloat16)
    key_rows = rotate(split_heads[:, 1], cos_table, sin_table).astype(jnp.bfloat16)
    values = split_heads[:, 2].astype(jnp.bfloat16)
    key_vals = jnp.stack(
        [key_rows.reshape(tok_rows, local_width), values.reshape(tok_rows, local_width)]
    )

    def attend(soft_state, kv_block, source):
        return forward_step(
            soft_state, kv_block, segments_from(source), queries, segment_local, scaling
        )

    start_state = (
        jnp.full((head_count, tok_rows), MASKED, jnp.float32),
        jnp.zeros((head_count, tok_rows), jnp.float32),
        jnp.zeros((head_count, tok_rows, HD), jnp.float32),
    )
    first_state = attend(start_state, key_vals, ctx_place)

    def pass_forward(step_index, carry):
        moving, soft_state = carry
        moving = shifted(moving, "ctx", 1)
        source = (ctx_place - step_index) % ctx_size
        return (moving, attend(soft_state, moving, source))

    _, soft_state = lax.fori_loop(1, ctx_size, pass_forward, (key_vals, first_state))
    maxima, totals, running = soft_state
    attended = running / totals[..., None]
    log_sums = maxima + jnp.log(totals)
    attn_low = (
        jnp.transpose(attended, (1, 0, 2)).reshape(tok_rows, local_width).astype(jnp.bfloat16)
    )
    attn_part = jnp.dot(attn_low, out_full, preferred_element_type=jnp.float32)
    middle = residual + lax.psum(attn_part.astype(jnp.bfloat16), "tp").astype(jnp.float32)
    mlp_gain, in_full, down_full = (
        lax.all_gather(g_mlp, "shard", axis=0, tiled=True),
        lax.all_gather(w_in, "shard", axis=0, tiled=True),
        lax.all_gather(w_mlp_out, "shard", axis=1, tiled=True),
    )
    normed_two, norm_two_back = jax.vjp(layer_norm, middle, mlp_gain.astype(jnp.float32))
    hidden_two = normed_two.astype(jnp.bfloat16)
    lifted = jnp.einsum("td,dcf->tcf", hidden_two, in_full, preferred_element_type=jnp.float32)
    mixed_f, geglu_back = jax.vjp(geglu, lifted)
    mixed_low = mixed_f.astype(jnp.bfloat16)
    mlp_part = jnp.dot(mixed_low, down_full, preferred_element_type=jnp.float32)
    output = (middle + lax.psum(mlp_part.astype(jnp.bfloat16), "tp").astype(jnp.float32)).astype(
        jnp.bfloat16
    )
    grad_down = jnp.einsum("tf,td->fd", mixed_low, cotangent, preferred_element_type=jnp.float32)
    grad_mixed = jnp.einsum("td,fd->tf", cotangent, down_full, preferred_element_type=jnp.float32)
    (grad_lifted,) = geglu_back(grad_mixed)
    lifted_low = grad_lifted.astype(jnp.bfloat16)
    grad_in = jnp.einsum("td,tcf->dcf", hidden_two, lifted_low, preferred_element_type=jnp.float32)
    hidden_two_part = jnp.einsum(
        "tcf,dcf->td", lifted_low, in_full, preferred_element_type=jnp.float32
    )
    grad_hidden_two = lax.psum(hidden_two_part.astype(jnp.bfloat16), "tp").astype(jnp.float32)
    grad_middle_norm, grad_mlp_gain = norm_two_back(grad_hidden_two)
    grad_middle = cotangent.astype(jnp.float32) + grad_middle_norm
    grad_branch = grad_middle.astype(jnp.bfloat16)
    grad_attn_out = jnp.einsum(
        "tn,td->nd", attn_low, grad_branch, preferred_element_type=jnp.float32
    )
    grad_attended = jnp.einsum(
        "td,nd->tn", grad_branch, out_full, preferred_element_type=jnp.float32
    ).astype(jnp.bfloat16)
    grad_heads = grad_attended.reshape(tok_rows, head_count, HD)
    row_delta = jnp.sum(
        jnp.transpose(grad_heads.astype(jnp.float32), (1, 0, 2)) * attended, axis=-1
    )

    def back_block(kv_block, source):
        return backward_step(
            kv_block,
            segments_from(source),
            queries,
            segment_local,
            grad_heads,
            log_sums,
            row_delta,
            scaling,
        )

    grad_query, grad_block = back_block(key_vals, ctx_place)

    def pass_backward(step_index, carry):
        moving, carried, grad_sofar = carry
        moving = shifted(moving, "ctx", 1)
        carried = shifted(carried.astype(jnp.bfloat16), "ctx", 1).astype(carried.dtype)
        source = (ctx_place - step_index) % ctx_size
        more_query, more_block = back_block(moving, source)
        return (moving, carried + more_block, grad_sofar + more_query)

    _, carried, grad_query = lax.fori_loop(
        1, ctx_size, pass_backward, (key_vals, grad_block, grad_query)
    )
    grad_keyvals = shifted(carried.astype(jnp.bfloat16), "ctx", 1).astype(carried.dtype)
    grad_keys = grad_keyvals[0].reshape(tok_rows, head_count, HD)
    grad_values = grad_keyvals[1].reshape(tok_rows, head_count, HD)
    grad_projected = jnp.stack(
        [
            rotate(grad_query, cos_table, -sin_table),
            rotate(grad_keys, cos_table, -sin_table),
            grad_values,
        ],
        axis=1,
    )
    grad_projected = grad_projected.reshape(tok_rows, 3, local_width).astype(jnp.bfloat16)
    grad_qkv = jnp.einsum(
        "td,tcn->dcn", hidden_one, grad_projected, preferred_element_type=jnp.float32
    )
    hidden_one_part = jnp.einsum(
        "tcn,dcn->td", grad_projected, qkv_full, preferred_element_type=jnp.float32
    )
    grad_hidden_one = lax.psum(hidden_one_part.astype(jnp.bfloat16), "tp").astype(jnp.float32)
    grad_input_norm, grad_attn_gain = norm_one_back(grad_hidden_one)
    grad_tokens = (grad_middle + grad_input_norm).astype(jnp.bfloat16)
    sharded = (
        lax.psum_scatter(
            grad_attn_gain.astype(jnp.bfloat16), "shard", scatter_dimension=0, tiled=True
        ).astype(jnp.float32),
        lax.psum_scatter(
            grad_qkv.astype(jnp.bfloat16), "shard", scatter_dimension=0, tiled=True
        ).astype(jnp.float32),
        lax.psum_scatter(
            grad_attn_out.astype(jnp.bfloat16), "shard", scatter_dimension=1, tiled=True
        ).astype(jnp.float32),
        lax.psum_scatter(
            grad_mlp_gain.astype(jnp.bfloat16), "shard", scatter_dimension=0, tiled=True
        ).astype(jnp.float32),
        lax.psum_scatter(
            grad_in.astype(jnp.bfloat16), "shard", scatter_dimension=0, tiled=True
        ).astype(jnp.float32),
        lax.psum_scatter(
            grad_down.astype(jnp.bfloat16), "shard", scatter_dimension=1, tiled=True
        ).astype(jnp.float32),
    )
    summed = (
        lax.psum(sharded[0].astype(jnp.bfloat16), "ctx").astype(jnp.float32),
        lax.psum(sharded[1].astype(jnp.bfloat16), "ctx").astype(jnp.float32),
        lax.psum(sharded[2].astype(jnp.bfloat16), "ctx").astype(jnp.float32),
        lax.psum(sharded[3].astype(jnp.bfloat16), "ctx").astype(jnp.float32),
        lax.psum(sharded[4].astype(jnp.bfloat16), "ctx").astype(jnp.float32),
        lax.psum(sharded[5].astype(jnp.bfloat16), "ctx").astype(jnp.float32),
    )
    return (output, grad_tokens, summed[0], summed[1], summed[2], summed[3], summed[4], summed[5])


LOG2E = 1.4426950408889634
VMEM_BYTES = 56 * 1024 * 1024


def rope_tables_t(places, head_size):
    half_size = head_size // 2
    powers = jnp.arange(half_size, dtype=jnp.float32) * (-2.0 * math.log(ROPE_BASE) / head_size)
    angles = jnp.exp(powers)[:, None] * places.astype(jnp.float32)[None, :]
    return (jnp.cos(angles), jnp.sin(angles))


def rotate_t(values, cos_t, sin_t):
    half_size = values.shape[-2] // 2
    front, back = values[..., :half_size, :], values[..., half_size:, :]
    return jnp.concatenate(
        [front * cos_t - back * sin_t, back * cos_t + front * sin_t], axis=-2
    )


def segment_ids(ends_ref, positions):
    ids = jnp.zeros(positions.shape, jnp.int32)
    for i in range(ends_ref.shape[1]):
        ids += (positions >= ends_ref[0, i]).astype(jnp.int32)
    return ids


def forward_kernel(blocks, ends_ref, q_ref, k_ref, v_ref, low_ref, out_ref, lse_ref, v_rows):
    step = pl.program_id(1)
    size = q_ref.shape[3]

    @pl.when(step == 0)
    def _():
        lane = lax.broadcasted_iota(jnp.int32, (size, HD), 1)
        ones = jnp.where(lane == 0, 1.0, 0.0).astype(jnp.bfloat16)
        for j in range(blocks):
            v_rows[j, :, :HD] = v_ref[j, 0].T
            v_rows[j, :, HD:] = ones

    queries = q_ref[0, 0].T
    scale = LOG2E / math.sqrt(HD)

    def run(masked):
        rows_id = None
        scores = []
        top = None
        for j in range(blocks):
            part = jnp.dot(queries, k_ref[j, 0], preferred_element_type=jnp.float32)
            if masked or j in (0, blocks - 1):
                if rows_id is None:
                    rows_id = segment_ids(
                        ends_ref, step * size + lax.broadcasted_iota(jnp.int32, (size, 1), 0)
                    )
                keys_id = segment_ids(
                    ends_ref, j * size + lax.broadcasted_iota(jnp.int32, (1, size), 1)
                )
                part = jnp.where(rows_id == keys_id, part, MASKED)
            scores.append(part)
            most = jnp.max(part, axis=1, keepdims=True)
            top = most if top is None else jnp.maximum(top, most)
        offset = top * scale
        total = None
        for j in range(blocks):
            raised = jnp.exp2(scores[j] * scale - offset).astype(jnp.bfloat16)
            part = jnp.dot(raised, v_rows[j], preferred_element_type=jnp.float32)
            total = part if total is None else total + part
        flat = total.T
        sums = flat[HD : HD + 1]
        result = flat[:HD] / sums
        out_ref[0, 0] = result
        low_ref[0, 0] = result.astype(jnp.bfloat16)
        lse_ref[0, 0] = offset.T + jnp.log2(sums)

    edge = (step == 0) | (step == blocks - 1)
    pl.when(edge)(lambda: run(True))
    pl.when(jnp.logical_not(edge))(lambda: run(False))


def backward_kernel(
    blocks, ends_ref, q_ref, k_ref, v_ref, do_ref, o_ref, lse_ref, grad_ref, k_rows, v_rows, dk, dv
):
    step = pl.program_id(1)
    size = q_ref.shape[3]

    @pl.when(step == 0)
    def _():
        for j in range(blocks):
            k_rows[j] = k_ref[j, 0].T
            v_rows[j] = v_ref[j, 0].T
        dk[...] = jnp.zeros_like(dk)
        dv[...] = jnp.zeros_like(dv)

    scale = LOG2E / math.sqrt(HD)
    queries_t = q_ref[0, 0]
    queries = queries_t.T
    grads_t = do_ref[0, 0]
    grads = grads_t.T
    delta = jnp.sum(grads_t.astype(jnp.float32) * o_ref[0, 0], axis=0, keepdims=True)
    lse = lse_ref[0, 0]

    def run(masked):
        dq = jnp.zeros((size, HD), jnp.float32)
        queries_id = None
        for j in range(blocks):
            scores = jnp.dot(k_rows[j], queries_t, preferred_element_type=jnp.float32)
            weights = jnp.exp2(scores * scale - lse)
            if masked or j in (0, blocks - 1):
                if queries_id is None:
                    queries_id = segment_ids(
                        ends_ref, step * size + lax.broadcasted_iota(jnp.int32, (1, size), 1)
                    )
                keys_id = segment_ids(
                    ends_ref, j * size + lax.broadcasted_iota(jnp.int32, (size, 1), 0)
                )
                weights = jnp.where(queries_id == keys_id, weights, 0.0)
            grad_weights = jnp.dot(v_rows[j], grads_t, preferred_element_type=jnp.float32)
            grad_scores = (weights * (grad_weights - delta)).astype(jnp.bfloat16)
            dv[j] += jnp.dot(
                weights.astype(jnp.bfloat16), grads, preferred_element_type=jnp.float32
            )
            dk[j] += jnp.dot(grad_scores, queries, preferred_element_type=jnp.float32)
            dq += lax.dot_general(
                grad_scores, k_rows[j], (((0,), (0,)), ((), ())), preferred_element_type=jnp.float32
            )
        grad_ref[step, 0, :HD] = (dq * (1.0 / math.sqrt(HD))).T.astype(jnp.bfloat16)

    edge = (step == 0) | (step == blocks - 1)
    pl.when(edge)(lambda: run(True))
    pl.when(jnp.logical_not(edge))(lambda: run(False))

    @pl.when(step == blocks - 1)
    def _():
        for j in range(blocks):
            grad_ref[j, 0, HD : 2 * HD] = (dk[j] * (1.0 / math.sqrt(HD))).T.astype(jnp.bfloat16)
            grad_ref[j, 0, 2 * HD :] = dv[j].T.astype(jnp.bfloat16)


def packed_specs(blocks, size):
    return [
        pl.BlockSpec(memory_space=pltpu.SMEM),
        pl.BlockSpec((1, 1, HD, size), lambda h, i: (i, h, 0, 0)),
        pl.BlockSpec((blocks, 1, HD, size), lambda h, i: (0, h, 1, 0)),
        pl.BlockSpec((blocks, 1, HD, size), lambda h, i: (0, h, 2, 0)),
    ]


def attention_forward(ends, packed):
    blocks, heads, _, size = packed.shape
    pairs = heads * (blocks * size) ** 2
    tile = pl.BlockSpec((1, 1, HD, size), lambda h, i: (i, h, 0, 0))
    line = pl.BlockSpec((1, 1, 1, size), lambda h, i: (i, h, 0, 0))
    return pl.pallas_call(
        functools.partial(forward_kernel, blocks),
        grid=(heads, blocks),
        in_specs=packed_specs(blocks, size),
        out_specs=[tile, tile, line],
        out_shape=[
            jax.ShapeDtypeStruct((blocks, heads, HD, size), jnp.bfloat16),
            jax.ShapeDtypeStruct((blocks, heads, HD, size), jnp.float32),
            jax.ShapeDtypeStruct((blocks, heads, 1, size), jnp.float32),
        ],
        scratch_shapes=[pltpu.VMEM((blocks, size, 2 * HD), jnp.bfloat16)],
        compiler_params=pltpu.CompilerParams(vmem_limit_bytes=VMEM_BYTES),
        cost_estimate=pl.CostEstimate(
            flops=16 * HD * pairs, bytes_accessed=packed.size * 6, transcendentals=pairs
        ),
        name="attention_forward",
    )(ends, packed, packed, packed)


def attention_backward(ends, packed, grads, attended, lse):
    blocks, heads, _, size = packed.shape
    pairs = heads * (blocks * size) ** 2
    tile = pl.BlockSpec((1, 1, HD, size), lambda h, i: (i, h, 0, 0))
    line = pl.BlockSpec((1, 1, 1, size), lambda h, i: (i, h, 0, 0))
    return pl.pallas_call(
        functools.partial(backward_kernel, blocks),
        grid=(heads, blocks),
        in_specs=packed_specs(blocks, size) + [tile, tile, line],
        out_specs=pl.BlockSpec((blocks, 1, 3 * HD, size), lambda h, i: (0, h, 0, 0)),
        out_shape=jax.ShapeDtypeStruct(packed.shape, jnp.bfloat16),
        scratch_shapes=[
            pltpu.VMEM((blocks, size, HD), jnp.bfloat16),
            pltpu.VMEM((blocks, size, HD), jnp.bfloat16),
            pltpu.VMEM((blocks, size, HD), jnp.float32),
            pltpu.VMEM((blocks, size, HD), jnp.float32),
        ],
        compiler_params=pltpu.CompilerParams(vmem_limit_bytes=VMEM_BYTES),
        cost_estimate=pl.CostEstimate(
            flops=40 * HD * pairs, bytes_accessed=packed.size * 10, transcendentals=pairs
        ),
        name="attention_backward",
    )(ends, packed, packed, packed, grads, attended, lse)


def exchanged(array_in):
    return lax.all_to_all(array_in, "ctx", split_axis=0, concat_axis=0, tiled=True)


def swapped(array_in, axis):
    return lax.ppermute(array_in, axis, [(0, 1), (1, 0)])


def gathered(block, dimension):
    if lax.axis_size("shard") != 2:
        return lax.all_gather(block, "shard", axis=dimension, tiled=True)
    other = swapped(block, "shard")
    return jnp.where(
        lax.axis_index("shard") == 0,
        jnp.concatenate([block, other], axis=dimension),
        jnp.concatenate([other, block], axis=dimension),
    )


def core_sum(partial):
    low = partial.astype(jnp.bfloat16)
    if lax.axis_size("tp") != 2:
        return lax.psum(low, "tp").astype(jnp.float32)
    return low.astype(jnp.float32) + swapped(low, "tp").astype(jnp.float32)


def owned_partial(product, cut, dimension, cut_axis):
    if lax.axis_size("shard") != 2:
        return lax.psum_scatter(
            product(cut).astype(jnp.bfloat16), "shard", scatter_dimension=dimension, tiled=True
        )
    half = cut.shape[cut_axis] // 2
    place = lax.axis_index("shard")
    theirs = lax.dynamic_slice_in_dim(cut, (1 - place) * half, half, cut_axis)
    mine = lax.dynamic_slice_in_dim(cut, place * half, half, cut_axis)
    arrived = swapped(product(theirs).astype(jnp.bfloat16), "shard")
    return (product(mine) + arrived.astype(jnp.float32)).astype(jnp.bfloat16)


def head_shards(tokens, cotangent, lengths, g_attn, w_qkv, w_attn_out, g_mlp, w_in, w_mlp_out):
    tok_rows = tokens.shape[0]
    ctx_size = lax.axis_size("ctx")
    ctx_place = lax.axis_index("ctx")
    row_index = jnp.arange(tok_rows, dtype=jnp.int32)
    _, inside = positions_of(lengths[0], ctx_place * tok_rows + row_index)
    cos_t, sin_t = rope_tables_t(inside, HD)
    ends = jnp.cumsum(lengths, axis=1).astype(jnp.int32)

    attn_gain = gathered(g_attn, 0)
    mlp_gain = gathered(g_mlp, 0)
    qkv_full = gathered(w_qkv, 0)
    w_in, w_mlp_out, w_attn_out, qkv_full = lax.optimization_barrier(
        (w_in, w_mlp_out, w_attn_out, qkv_full)
    )
    out_full = gathered(w_attn_out, 1)
    in_full = gathered(w_in, 0)
    down_full = gathered(w_mlp_out, 1)
    residual = tokens.astype(jnp.float32)
    normed_one, norm_one_back = jax.vjp(layer_norm, residual, attn_gain.astype(jnp.float32))
    hidden_one = normed_one.astype(jnp.bfloat16)
    projected = jnp.einsum("td,dcn->cnt", hidden_one, qkv_full, preferred_element_type=jnp.float32)
    local_width = projected.shape[1]
    head_count = local_width // HD
    own_heads = head_count // ctx_size
    split_heads = projected.reshape(3, head_count, HD, tok_rows)
    packed = jnp.concatenate(
        [
            rotate_t(split_heads[0], cos_t, sin_t).astype(jnp.bfloat16),
            rotate_t(split_heads[1], cos_t, sin_t).astype(jnp.bfloat16),
            split_heads[2].astype(jnp.bfloat16),
        ],
        axis=1,
    ).reshape(ctx_size, own_heads, 3 * HD, tok_rows)
    packed = exchanged(packed)
    own_low, own_attended, lse = attention_forward(ends, packed)
    own_low, in_full, out_full = lax.optimization_barrier((own_low, in_full, out_full))
    attn_low = exchanged(own_low).reshape(local_width, tok_rows)
    attn_part = jnp.einsum("nt,nd->td", attn_low, out_full, preferred_element_type=jnp.float32)
    middle = residual + core_sum(attn_part)
    normed_two, norm_two_back = jax.vjp(layer_norm, middle, mlp_gain.astype(jnp.float32))
    hidden_two = normed_two.astype(jnp.bfloat16)
    lifted = jnp.einsum("td,dcf->tcf", hidden_two, in_full, preferred_element_type=jnp.float32)
    mixed_f, geglu_back = jax.vjp(geglu, lifted)
    mixed_low = mixed_f.astype(jnp.bfloat16)
    mlp_part = jnp.dot(mixed_low, down_full, preferred_element_type=jnp.float32)
    output = (middle + core_sum(mlp_part)).astype(jnp.bfloat16)
    part_down = owned_partial(
        lambda cut: jnp.einsum("tf,td->fd", mixed_low, cut, preferred_element_type=jnp.float32),
        cotangent,
        1,
        1,
    )
    grad_mixed = jnp.einsum("td,fd->tf", cotangent, down_full, preferred_element_type=jnp.float32)
    (grad_lifted,) = geglu_back(grad_mixed)
    lifted_low = grad_lifted.astype(jnp.bfloat16)
    part_in = owned_partial(
        lambda cut: jnp.einsum("td,tcf->dcf", cut, lifted_low, preferred_element_type=jnp.float32),
        hidden_two,
        0,
        1,
    )
    hidden_two_part = jnp.einsum(
        "tcf,dcf->td", lifted_low, in_full, preferred_element_type=jnp.float32
    )
    grad_middle_norm, grad_mlp_gain = norm_two_back(core_sum(hidden_two_part))
    grad_middle = cotangent.astype(jnp.float32) + grad_middle_norm
    grad_branch = grad_middle.astype(jnp.bfloat16)
    part_out = owned_partial(
        lambda cut: jnp.einsum("nt,td->nd", attn_low, cut, preferred_element_type=jnp.float32),
        grad_branch,
        1,
        1,
    )
    grad_attended = jnp.einsum(
        "td,nd->nt", grad_branch, out_full, preferred_element_type=jnp.float32
    ).astype(jnp.bfloat16)
    own_grads = exchanged(grad_attended.reshape(ctx_size, own_heads, HD, tok_rows))
    summed_early = lax.psum((part_in, part_down, part_out), "ctx")
    own_packed = attention_backward(ends, packed, own_grads, own_attended, lse)
    grad_packed = exchanged(own_packed).reshape(head_count, 3, HD, tok_rows)
    grad_projected = jnp.stack(
        [
            rotate_t(grad_packed[:, 0].astype(jnp.float32), cos_t, -sin_t).astype(jnp.bfloat16),
            rotate_t(grad_packed[:, 1].astype(jnp.float32), cos_t, -sin_t).astype(jnp.bfloat16),
            grad_packed[:, 2],
        ],
        axis=0,
    ).reshape(3, local_width, tok_rows)
    part_qkv = owned_partial(
        lambda cut: jnp.einsum(
            "td,cnt->dcn", cut, grad_projected, preferred_element_type=jnp.float32
        ),
        hidden_one,
        0,
        1,
    )
    hidden_one_part = jnp.einsum(
        "cnt,dcn->td", grad_projected, qkv_full, preferred_element_type=jnp.float32
    )
    grad_input_norm, grad_attn_gain = norm_one_back(core_sum(hidden_one_part))
    grad_tokens = (grad_middle + grad_input_norm).astype(jnp.bfloat16)
    gains = lax.psum_scatter(
        jnp.stack([grad_attn_gain, grad_mlp_gain]).astype(jnp.bfloat16),
        "shard",
        scatter_dimension=1,
        tiled=True,
    )
    part_qkv, gains, summed_early = lax.optimization_barrier((part_qkv, gains, summed_early))
    summed_qkv, gains = lax.psum((part_qkv, gains), "ctx")
    return (
        output,
        grad_tokens,
        gains[0].astype(jnp.float32),
        summed_qkv.astype(jnp.float32),
        summed_early[2].astype(jnp.float32),
        gains[1].astype(jnp.float32),
        summed_early[0].astype(jnp.float32),
        summed_early[1].astype(jnp.float32),
    )


def layer(tokens, cotangent, lengths, g_attn, w_qkv, w_attn_out, g_mlp, w_in, w_mlp_out):
    head_count = w_qkv.shape[2] // HD
    whole_heads = head_count % lax.axis_size("ctx") == 0
    return (head_shards if whole_heads else shards)(
        tokens, cotangent, lengths, g_attn, w_qkv, w_attn_out, g_mlp, w_in, w_mlp_out
    )


def solution(mesh):
    return jax.shard_map(
        layer,
        mesh=mesh,
        in_specs=(
            P(("shard", "ctx"), None),
            P(("shard", "ctx"), None),
            P("shard", None),
            P("shard"),
            P("shard", None, "tp"),
            P("tp", "shard"),
            P("shard"),
            P("shard", None, "tp"),
            P("tp", "shard"),
        ),
        out_specs=(
            P(("shard", "ctx"), None),
            P(("shard", "ctx"), None),
            P("shard"),
            P("shard", None, "tp"),
            P("tp", "shard"),
            P("shard"),
            P("shard", None, "tp"),
            P("tp", "shard"),
        ),
        check_vma=False,
    )
```

```python
import functools
import math

import jax
import jax.numpy as jnp
from jax import lax
from jax.experimental import pallas as pl
from jax.experimental.pallas import tpu as pltpu
from jax.sharding import PartitionSpec as P

HD = 64


EPSILON = 1e-05
ROPE_BASE = 160000.0
MASKED = -1e30


def shifted(block, axis, distance):
    devices = range(lax.axis_size(axis))
    route = [((i - distance) % len(devices), i) for i in devices]
    return lax.ppermute(block, axis, route)


def layer_norm(values, norm_gain):
    average = jnp.mean(values, axis=-1, keepdims=True)
    centred = values - average
    spread = jnp.mean(centred * centred, axis=-1, keepdims=True)
    return centred * lax.rsqrt(spread + EPSILON) * norm_gain


def rotate(values, cos_table, sin_table):
    half_size = values.shape[-1] // 2
    front_half = values[..., :half_size]
    back_half = values[..., half_size:]
    cos_rows = cos_table[:, None, :]
    sin_rows = sin_table[:, None, :]
    return jnp.concatenate(
        [
            front_half * cos_rows - back_half * sin_rows,
            back_half * cos_rows + front_half * sin_rows,
        ],
        axis=-1,
    )


def rope_tables(places, head_size):
    half_size = head_size // 2
    powers = jnp.arange(half_size, dtype=jnp.float32) * (-2.0 * math.log(ROPE_BASE) / head_size)
    angles = places.astype(jnp.float32)[:, None] * jnp.exp(powers)[None, :]
    return (jnp.cos(angles), jnp.sin(angles))


def positions_of(seq_lengths, places):
    seq_count = seq_lengths.shape[0]
    seq_ends = jnp.cumsum(seq_lengths)
    seq_starts = seq_ends - seq_lengths
    segment = jnp.sum((places[:, None] >= seq_ends[None, :]).astype(jnp.int32), axis=1)
    chosen = segment[:, None] == jnp.arange(seq_count, dtype=jnp.int32)[None, :]
    seq_first = jnp.sum(jnp.where(chosen, seq_starts[None, :], 0), axis=1)
    return (segment, places - seq_first)


def geglu(lifted):
    return jax.nn.gelu(lifted[:, 0], approximate=False) * lifted[:, 1]


def split_block(kv_block, head_count):
    key_count = kv_block.shape[1]
    return (
        kv_block[0].reshape(key_count, head_count, -1),
        kv_block[1].reshape(key_count, head_count, -1),
    )


def masked_scores(queries, key_rows, seg_query, seg_keys, scaling):
    scores = (
        jnp.einsum("qhd,khd->hqk", queries, key_rows, preferred_element_type=jnp.float32) * scaling
    )
    same_seg = (seg_query[:, None] == seg_keys[None, :])[None]
    return (jnp.where(same_seg, scores, MASKED), same_seg)


def forward_step(soft_state, kv_block, seg_keys, queries, seg_query, scaling):
    maxima, totals, running = soft_state
    key_rows, values = split_block(kv_block, queries.shape[1])
    scores, same_seg = masked_scores(queries, key_rows, seg_query, seg_keys, scaling)
    new_max = jnp.maximum(maxima, jnp.max(scores, axis=-1))
    weights = jnp.where(same_seg, jnp.exp(scores - new_max[..., None]), 0.0)
    factor = jnp.exp(maxima - new_max)
    totals = totals * factor + jnp.sum(weights, axis=-1)
    update = jnp.einsum(
        "hqk,khd->hqd", weights.astype(jnp.bfloat16), values, preferred_element_type=jnp.float32
    )
    return (new_max, totals, running * factor[..., None] + update)


def backward_step(kv_block, seg_keys, queries, seg_query, grad_heads, log_sums, row_delta, scaling):
    key_rows, values = split_block(kv_block, queries.shape[1])
    scores, same_seg = masked_scores(queries, key_rows, seg_query, seg_keys, scaling)
    weights = jnp.where(same_seg, jnp.exp(scores - log_sums[..., None]), 0.0)
    grad_weights = jnp.einsum(
        "qhd,khd->hqk", grad_heads, values, preferred_element_type=jnp.float32
    )
    grad_scores = (weights * (grad_weights - row_delta[..., None])).astype(jnp.bfloat16)
    grad_query = (
        jnp.einsum("hqk,khd->qhd", grad_scores, key_rows, preferred_element_type=jnp.float32)
        * scaling
    )
    grad_keys = (
        jnp.einsum("hqk,qhd->khd", grad_scores, queries, preferred_element_type=jnp.float32)
        * scaling
    )
    grad_values = jnp.einsum(
        "hqk,qhd->khd", weights.astype(jnp.bfloat16), grad_heads, preferred_element_type=jnp.float32
    )
    key_count = key_rows.shape[0]
    return (
        grad_query,
        jnp.stack([grad_keys.reshape(key_count, -1), grad_values.reshape(key_count, -1)]),
    )


def shards(tokens, cotangent, lengths, g_attn, w_qkv, w_attn_out, g_mlp, w_in, w_mlp_out):
    tok_rows = tokens.shape[0]
    ctx_size = lax.axis_size("ctx")
    ctx_place = lax.axis_index("ctx")
    seq_lengths = lengths[0]
    row_index = jnp.arange(tok_rows, dtype=jnp.int32)
    segment_local, inside = positions_of(seq_lengths, ctx_place * tok_rows + row_index)
    cos_table, sin_table = rope_tables(inside, HD)
    scaling = 1.0 / math.sqrt(HD)

    def segments_from(source):
        return positions_of(seq_lengths, source * tok_rows + row_index)[0]

    attn_gain, qkv_full, out_full = (
        lax.all_gather(g_attn, "shard", axis=0, tiled=True),
        lax.all_gather(w_qkv, "shard", axis=0, tiled=True),
        lax.all_gather(w_attn_out, "shard", axis=1, tiled=True),
    )
    residual = tokens.astype(jnp.float32)
    normed_one, norm_one_back = jax.vjp(layer_norm, residual, attn_gain.astype(jnp.float32))
    hidden_one = normed_one.astype(jnp.bfloat16)
    projected = jnp.einsum("td,dcn->tcn", hidden_one, qkv_full, preferred_element_type=jnp.float32)
    local_width = projected.shape[2]
    head_count = local_width // HD
    split_heads = projected.reshape(tok_rows, 3, head_count, HD)
    queries = rotate(split_heads[:, 0], cos_table, sin_table).astype(jnp.bfloat16)
    key_rows = rotate(split_heads[:, 1], cos_table, sin_table).astype(jnp.bfloat16)
    values = split_heads[:, 2].astype(jnp.bfloat16)
    key_vals = jnp.stack(
        [key_rows.reshape(tok_rows, local_width), values.reshape(tok_rows, local_width)]
    )

    def attend(soft_state, kv_block, source):
        return forward_step(
            soft_state, kv_block, segments_from(source), queries, segment_local, scaling
        )

    start_state = (
        jnp.full((head_count, tok_rows), MASKED, jnp.float32),
        jnp.zeros((head_count, tok_rows), jnp.float32),
        jnp.zeros((head_count, tok_rows, HD), jnp.float32),
    )
    first_state = attend(start_state, key_vals, ctx_place)

    def pass_forward(step_index, carry):
        moving, soft_state = carry
        moving = shifted(moving, "ctx", 1)
        source = (ctx_place - step_index) % ctx_size
        return (moving, attend(soft_state, moving, source))

    _, soft_state = lax.fori_loop(1, ctx_size, pass_forward, (key_vals, first_state))
    maxima, totals, running = soft_state
    attended = running / totals[..., None]
    log_sums = maxima + jnp.log(totals)
    attn_low = (
        jnp.transpose(attended, (1, 0, 2)).reshape(tok_rows, local_width).astype(jnp.bfloat16)
    )
    attn_part = jnp.dot(attn_low, out_full, preferred_element_type=jnp.float32)
    middle = residual + lax.psum(attn_part.astype(jnp.bfloat16), "tp").astype(jnp.float32)
    mlp_gain, in_full, down_full = (
        lax.all_gather(g_mlp, "shard", axis=0, tiled=True),
        lax.all_gather(w_in, "shard", axis=0, tiled=True),
        lax.all_gather(w_mlp_out, "shard", axis=1, tiled=True),
    )
    normed_two, norm_two_back = jax.vjp(layer_norm, middle, mlp_gain.astype(jnp.float32))
    hidden_two = normed_two.astype(jnp.bfloat16)
    lifted = jnp.einsum("td,dcf->tcf", hidden_two, in_full, preferred_element_type=jnp.float32)
    mixed_f, geglu_back = jax.vjp(geglu, lifted)
    mixed_low = mixed_f.astype(jnp.bfloat16)
    mlp_part = jnp.dot(mixed_low, down_full, preferred_element_type=jnp.float32)
    output = (middle + lax.psum(mlp_part.astype(jnp.bfloat16), "tp").astype(jnp.float32)).astype(
        jnp.bfloat16
    )
    grad_down = jnp.einsum("tf,td->fd", mixed_low, cotangent, preferred_element_type=jnp.float32)
    grad_mixed = jnp.einsum("td,fd->tf", cotangent, down_full, preferred_element_type=jnp.float32)
    (grad_lifted,) = geglu_back(grad_mixed)
    lifted_low = grad_lifted.astype(jnp.bfloat16)
    grad_in = jnp.einsum("td,tcf->dcf", hidden_two, lifted_low, preferred_element_type=jnp.float32)
    hidden_two_part = jnp.einsum(
        "tcf,dcf->td", lifted_low, in_full, preferred_element_type=jnp.float32
    )
    grad_hidden_two = lax.psum(hidden_two_part.astype(jnp.bfloat16), "tp").astype(jnp.float32)
    grad_middle_norm, grad_mlp_gain = norm_two_back(grad_hidden_two)
    grad_middle = cotangent.astype(jnp.float32) + grad_middle_norm
    grad_branch = grad_middle.astype(jnp.bfloat16)
    grad_attn_out = jnp.einsum(
        "tn,td->nd", attn_low, grad_branch, preferred_element_type=jnp.float32
    )
    grad_attended = jnp.einsum(
        "td,nd->tn", grad_branch, out_full, preferred_element_type=jnp.float32
    ).astype(jnp.bfloat16)
    grad_heads = grad_attended.reshape(tok_rows, head_count, HD)
    row_delta = jnp.sum(
        jnp.transpose(grad_heads.astype(jnp.float32), (1, 0, 2)) * attended, axis=-1
    )

    def back_block(kv_block, source):
        return backward_step(
            kv_block,
            segments_from(source),
            queries,
            segment_local,
            grad_heads,
            log_sums,
            row_delta,
            scaling,
        )

    grad_query, grad_block = back_block(key_vals, ctx_place)

    def pass_backward(step_index, carry):
        moving, carried, grad_sofar = carry
        moving = shifted(moving, "ctx", 1)
        carried = shifted(carried.astype(jnp.bfloat16), "ctx", 1).astype(carried.dtype)
        source = (ctx_place - step_index) % ctx_size
        more_query, more_block = back_block(moving, source)
        return (moving, carried + more_block, grad_sofar + more_query)

    _, carried, grad_query = lax.fori_loop(
        1, ctx_size, pass_backward, (key_vals, grad_block, grad_query)
    )
    grad_keyvals = shifted(carried.astype(jnp.bfloat16), "ctx", 1).astype(carried.dtype)
    grad_keys = grad_keyvals[0].reshape(tok_rows, head_count, HD)
    grad_values = grad_keyvals[1].reshape(tok_rows, head_count, HD)
    grad_projected = jnp.stack(
        [
            rotate(grad_query, cos_table, -sin_table),
            rotate(grad_keys, cos_table, -sin_table),
            grad_values,
        ],
        axis=1,
    )
    grad_projected = grad_projected.reshape(tok_rows, 3, local_width).astype(jnp.bfloat16)
    grad_qkv = jnp.einsum(
        "td,tcn->dcn", hidden_one, grad_projected, preferred_element_type=jnp.float32
    )
    hidden_one_part = jnp.einsum(
        "tcn,dcn->td", grad_projected, qkv_full, preferred_element_type=jnp.float32
    )
    grad_hidden_one = lax.psum(hidden_one_part.astype(jnp.bfloat16), "tp").astype(jnp.float32)
    grad_input_norm, grad_attn_gain = norm_one_back(grad_hidden_one)
    grad_tokens = (grad_middle + grad_input_norm).astype(jnp.bfloat16)
    sharded = (
        lax.psum_scatter(
            grad_attn_gain.astype(jnp.bfloat16), "shard", scatter_dimension=0, tiled=True
        ).astype(jnp.float32),
        lax.psum_scatter(
            grad_qkv.astype(jnp.bfloat16), "shard", scatter_dimension=0, tiled=True
        ).astype(jnp.float32),
        lax.psum_scatter(
            grad_attn_out.astype(jnp.bfloat16), "shard", scatter_dimension=1, tiled=True
        ).astype(jnp.float32),
        lax.psum_scatter(
            grad_mlp_gain.astype(jnp.bfloat16), "shard", scatter_dimension=0, tiled=True
        ).astype(jnp.float32),
        lax.psum_scatter(
            grad_in.astype(jnp.bfloat16), "shard", scatter_dimension=0, tiled=True
        ).astype(jnp.float32),
        lax.psum_scatter(
            grad_down.astype(jnp.bfloat16), "shard", scatter_dimension=1, tiled=True
        ).astype(jnp.float32),
    )
    summed = (
        lax.psum(sharded[0].astype(jnp.bfloat16), "ctx").astype(jnp.float32),
        lax.psum(sharded[1].astype(jnp.bfloat16), "ctx").astype(jnp.float32),
        lax.psum(sharded[2].astype(jnp.bfloat16), "ctx").astype(jnp.float32),
        lax.psum(sharded[3].astype(jnp.bfloat16), "ctx").astype(jnp.float32),
        lax.psum(sharded[4].astype(jnp.bfloat16), "ctx").astype(jnp.float32),
        lax.psum(sharded[5].astype(jnp.bfloat16), "ctx").astype(jnp.float32),
    )
    return (output, grad_tokens, summed[0], summed[1], summed[2], summed[3], summed[4], summed[5])


LOG2E = 1.4426950408889634
RING = [0, 2, 4, 6, 7, 5, 3, 1]
VMEM_BYTES = 56 * 1024 * 1024


def rope_tables_t(places, head_size):
    half_size = head_size // 2
    powers = jnp.arange(half_size, dtype=jnp.float32) * (-2.0 * math.log(ROPE_BASE) / head_size)
    angles = jnp.exp(powers)[:, None] * places.astype(jnp.float32)[None, :]
    return (jnp.cos(angles), jnp.sin(angles))


def rotate_t(values, cos_t, sin_t):
    half_size = values.shape[-2] // 2
    front, back = values[..., :half_size, :], values[..., half_size:, :]
    return jnp.concatenate(
        [front * cos_t - back * sin_t, back * cos_t + front * sin_t], axis=-2
    )


def segment_ids(ends_ref, positions):
    ids = jnp.zeros(positions.shape, jnp.int32)
    for i in range(ends_ref.shape[1]):
        ids += (positions >= ends_ref[0, i]).astype(jnp.int32)
    return ids


def forward_kernel(blocks, ends_ref, q_ref, k_ref, v_ref, low_ref, out_ref, lse_ref, v_rows):
    step = pl.program_id(1)
    size = q_ref.shape[3]

    @pl.when(step == 0)
    def _():
        lane = lax.broadcasted_iota(jnp.int32, (size, HD), 1)
        ones = jnp.where(lane == 0, 1.0, 0.0).astype(jnp.bfloat16)
        for j in range(blocks):
            v_rows[j, :, :HD] = v_ref[j, 0].T
            v_rows[j, :, HD:] = ones

    queries = q_ref[0, 0].T
    scale = LOG2E / math.sqrt(HD)

    def run(masked):
        rows_id = None
        scores = []
        top = None
        for j in range(blocks):
            part = jnp.dot(queries, k_ref[j, 0], preferred_element_type=jnp.float32)
            if masked or j in (0, blocks - 1):
                if rows_id is None:
                    rows_id = segment_ids(
                        ends_ref, step * size + lax.broadcasted_iota(jnp.int32, (size, 1), 0)
                    )
                keys_id = segment_ids(
                    ends_ref, j * size + lax.broadcasted_iota(jnp.int32, (1, size), 1)
                )
                part = jnp.where(rows_id == keys_id, part, MASKED)
            scores.append(part)
            most = jnp.max(part, axis=1, keepdims=True)
            top = most if top is None else jnp.maximum(top, most)
        offset = top * scale
        total = None
        for j in range(blocks):
            raised = jnp.exp2(scores[j] * scale - offset).astype(jnp.bfloat16)
            part = jnp.dot(raised, v_rows[j], preferred_element_type=jnp.float32)
            total = part if total is None else total + part
        flat = total.T
        sums = flat[HD : HD + 1]
        result = flat[:HD] / sums
        out_ref[0, 0] = result
        low_ref[0, 0] = result.astype(jnp.bfloat16)
        lse_ref[0, 0] = offset.T + jnp.log2(sums)

    edge = (step == 0) | (step == blocks - 1)
    pl.when(edge)(lambda: run(True))
    pl.when(jnp.logical_not(edge))(lambda: run(False))


def backward_kernel(
    blocks, ends_ref, q_ref, k_ref, v_ref, do_ref, o_ref, lse_ref, grad_ref, k_rows, v_rows, dk, dv
):
    step = pl.program_id(1)
    size = q_ref.shape[3]

    @pl.when(step == 0)
    def _():
        for j in range(blocks):
            k_rows[j] = k_ref[j, 0].T
            v_rows[j] = v_ref[j, 0].T
        dk[...] = jnp.zeros_like(dk)
        dv[...] = jnp.zeros_like(dv)

    scale = LOG2E / math.sqrt(HD)
    queries_t = q_ref[0, 0]
    queries = queries_t.T
    grads_t = do_ref[0, 0]
    grads = grads_t.T
    delta = jnp.sum(grads_t.astype(jnp.float32) * o_ref[0, 0], axis=0, keepdims=True)
    lse = lse_ref[0, 0]

    def run(masked):
        dq = jnp.zeros((size, HD), jnp.float32)
        queries_id = None
        for j in range(blocks):
            scores = jnp.dot(k_rows[j], queries_t, preferred_element_type=jnp.float32)
            weights = jnp.exp2(scores * scale - lse)
            if masked or j in (0, blocks - 1):
                if queries_id is None:
                    queries_id = segment_ids(
                        ends_ref, step * size + lax.broadcasted_iota(jnp.int32, (1, size), 1)
                    )
                keys_id = segment_ids(
                    ends_ref, j * size + lax.broadcasted_iota(jnp.int32, (size, 1), 0)
                )
                weights = jnp.where(queries_id == keys_id, weights, 0.0)
            grad_weights = jnp.dot(v_rows[j], grads_t, preferred_element_type=jnp.float32)
            grad_scores = (weights * (grad_weights - delta)).astype(jnp.bfloat16)
            dv[j] += jnp.dot(
                weights.astype(jnp.bfloat16), grads, preferred_element_type=jnp.float32
            )
            dk[j] += jnp.dot(grad_scores, queries, preferred_element_type=jnp.float32)
            dq += lax.dot_general(
                grad_scores, k_rows[j], (((0,), (0,)), ((), ())), preferred_element_type=jnp.float32
            )
        grad_ref[step, 0, :HD] = (dq * (1.0 / math.sqrt(HD))).T.astype(jnp.bfloat16)

    edge = (step == 0) | (step == blocks - 1)
    pl.when(edge)(lambda: run(True))
    pl.when(jnp.logical_not(edge))(lambda: run(False))

    @pl.when(step == blocks - 1)
    def _():
        for j in range(blocks):
            grad_ref[j, 0, HD : 2 * HD] = (dk[j] * (1.0 / math.sqrt(HD))).T.astype(jnp.bfloat16)
            grad_ref[j, 0, 2 * HD :] = dv[j].T.astype(jnp.bfloat16)


def packed_specs(blocks, size):
    return [
        pl.BlockSpec(memory_space=pltpu.SMEM),
        pl.BlockSpec((1, 1, HD, size), lambda h, i: (i, h, 0, 0)),
        pl.BlockSpec((blocks, 1, HD, size), lambda h, i: (0, h, 1, 0)),
        pl.BlockSpec((blocks, 1, HD, size), lambda h, i: (0, h, 2, 0)),
    ]


def attention_forward(ends, packed):
    blocks, heads, _, size = packed.shape
    pairs = heads * (blocks * size) ** 2
    tile = pl.BlockSpec((1, 1, HD, size), lambda h, i: (i, h, 0, 0))
    line = pl.BlockSpec((1, 1, 1, size), lambda h, i: (i, h, 0, 0))
    return pl.pallas_call(
        functools.partial(forward_kernel, blocks),
        grid=(heads, blocks),
        in_specs=packed_specs(blocks, size),
        out_specs=[tile, tile, line],
        out_shape=[
            jax.ShapeDtypeStruct((blocks, heads, HD, size), jnp.bfloat16),
            jax.ShapeDtypeStruct((blocks, heads, HD, size), jnp.float32),
            jax.ShapeDtypeStruct((blocks, heads, 1, size), jnp.float32),
        ],
        scratch_shapes=[pltpu.VMEM((blocks, size, 2 * HD), jnp.bfloat16)],
        compiler_params=pltpu.CompilerParams(vmem_limit_bytes=VMEM_BYTES),
        cost_estimate=pl.CostEstimate(
            flops=16 * HD * pairs, bytes_accessed=packed.size * 6, transcendentals=pairs
        ),
        name="attention_forward",
    )(ends, packed, packed, packed)


def attention_backward(ends, packed, grads, attended, lse):
    blocks, heads, _, size = packed.shape
    pairs = heads * (blocks * size) ** 2
    tile = pl.BlockSpec((1, 1, HD, size), lambda h, i: (i, h, 0, 0))
    line = pl.BlockSpec((1, 1, 1, size), lambda h, i: (i, h, 0, 0))
    return pl.pallas_call(
        functools.partial(backward_kernel, blocks),
        grid=(heads, blocks),
        in_specs=packed_specs(blocks, size) + [tile, tile, line],
        out_specs=pl.BlockSpec((blocks, 1, 3 * HD, size), lambda h, i: (0, h, 0, 0)),
        out_shape=jax.ShapeDtypeStruct(packed.shape, jnp.bfloat16),
        scratch_shapes=[
            pltpu.VMEM((blocks, size, HD), jnp.bfloat16),
            pltpu.VMEM((blocks, size, HD), jnp.bfloat16),
            pltpu.VMEM((blocks, size, HD), jnp.float32),
            pltpu.VMEM((blocks, size, HD), jnp.float32),
        ],
        compiler_params=pltpu.CompilerParams(vmem_limit_bytes=VMEM_BYTES),
        cost_estimate=pl.CostEstimate(
            flops=40 * HD * pairs, bytes_accessed=packed.size * 10, transcendentals=pairs
        ),
        name="attention_backward",
    )(ends, packed, packed, packed, grads, attended, lse)


def exchanged(array_in):
    return lax.all_to_all(array_in, "ctx", split_axis=0, concat_axis=0, tiled=True)


def swapped(array_in, axis):
    return lax.ppermute(array_in, axis, [(0, 1), (1, 0)])


def joined(block, other, dimension):
    return jnp.where(
        lax.axis_index("shard") == 0,
        jnp.concatenate([block, other], axis=dimension),
        jnp.concatenate([other, block], axis=dimension),
    )


def halves(array_in, axis):
    half = array_in.shape[axis] // 2
    place = lax.axis_index("shard")
    return (
        lax.dynamic_slice_in_dim(array_in, place * half, half, axis),
        lax.dynamic_slice_in_dim(array_in, (1 - place) * half, half, axis),
    )


def added(product, arrived):
    return (product + arrived.astype(jnp.float32)).astype(jnp.bfloat16)


def core_sum(partial):
    low = partial.astype(jnp.bfloat16)
    return low.astype(jnp.float32) + swapped(low, "tp").astype(jnp.float32)


def block_sum(partial):
    size = lax.axis_size("ctx")
    place = lax.axis_index("ctx")
    pieces = exchanged(partial)
    total = jnp.sum(pieces.astype(jnp.float32), axis=0).astype(jnp.bfloat16)
    order = RING if size == len(RING) else list(range(size))
    spots = [0] * size
    for i in range(size):
        spots[order[i]] = i
    spot = jnp.array(spots, jnp.int32)[place]
    ring = jnp.array(order, jnp.int32)
    result = jnp.zeros((size,) + total.shape, jnp.bfloat16)
    result = lax.dynamic_update_slice_in_dim(result, total[None], place, 0)
    right, left = total, total
    for step in range(1, size // 2 + 1):
        forward = [(order[i], order[(i + 1) % size]) for i in range(size)]
        right = lax.ppermute(right, "ctx", forward)
        source = ring[(spot - step) % size]
        result = lax.dynamic_update_slice_in_dim(result, right[None], source, 0)
        if step < size - step:
            left = lax.ppermute(left, "ctx", [(d, s) for s, d in forward])
            source = ring[(spot + step) % size]
            result = lax.dynamic_update_slice_in_dim(result, left[None], source, 0)
    return result


def head_shards(tokens, cotangent, lengths, g_attn, w_qkv, w_attn_out, g_mlp, w_in, w_mlp_out):
    tok_rows = tokens.shape[0]
    ctx_size = lax.axis_size("ctx")
    ctx_place = lax.axis_index("ctx")
    row_index = jnp.arange(tok_rows, dtype=jnp.int32)
    _, inside = positions_of(lengths[0], ctx_place * tok_rows + row_index)
    cos_t, sin_t = rope_tables_t(inside, HD)
    ends = jnp.cumsum(lengths, axis=1).astype(jnp.int32)

    attn_gain = joined(g_attn, swapped(g_attn, "shard"), 0)
    mlp_gain = joined(g_mlp, swapped(g_mlp, "shard"), 0)
    qkv_other = swapped(w_qkv, "shard")
    w_in, w_mlp_out, w_attn_out, qkv_other = lax.optimization_barrier(
        (w_in, w_mlp_out, w_attn_out, qkv_other)
    )
    qkv_full = joined(w_qkv, qkv_other, 0)
    out_other = swapped(w_attn_out, "shard")
    in_other = swapped(w_in, "shard")
    down_other = swapped(w_mlp_out, "shard")
    residual = tokens.astype(jnp.float32)
    normed_one, norm_one_back = jax.vjp(layer_norm, residual, attn_gain.astype(jnp.float32))
    hidden_one = normed_one.astype(jnp.bfloat16)
    projected = jnp.einsum("td,dcn->cnt", hidden_one, qkv_full, preferred_element_type=jnp.float32)
    local_width = projected.shape[1]
    head_count = local_width // HD
    own_heads = head_count // ctx_size
    split_heads = projected.reshape(3, head_count, HD, tok_rows)
    packed = jnp.concatenate(
        [
            rotate_t(split_heads[0], cos_t, sin_t).astype(jnp.bfloat16),
            rotate_t(split_heads[1], cos_t, sin_t).astype(jnp.bfloat16),
            split_heads[2].astype(jnp.bfloat16),
        ],
        axis=1,
    ).reshape(ctx_size, own_heads, 3 * HD, tok_rows)
    packed = exchanged(packed)
    own_low, own_attended, lse = attention_forward(ends, packed)
    own_low, in_other, out_other = lax.optimization_barrier((own_low, in_other, out_other))
    out_full = joined(w_attn_out, out_other, 1)
    in_full = joined(w_in, in_other, 0)
    down_full = joined(w_mlp_out, down_other, 1)
    attn_low = exchanged(own_low).reshape(local_width, tok_rows)
    attn_part = jnp.einsum("nt,nd->td", attn_low, out_full, preferred_element_type=jnp.float32)
    middle = residual + core_sum(attn_part)
    normed_two, norm_two_back = jax.vjp(layer_norm, middle, mlp_gain.astype(jnp.float32))
    hidden_two = normed_two.astype(jnp.bfloat16)
    lifted = jnp.einsum("td,dcf->tcf", hidden_two, in_full, preferred_element_type=jnp.float32)
    mixed_f, geglu_back = jax.vjp(geglu, lifted)
    mixed_low = mixed_f.astype(jnp.bfloat16)
    mlp_part = jnp.dot(mixed_low, down_full, preferred_element_type=jnp.float32)
    output = (middle + core_sum(mlp_part)).astype(jnp.bfloat16)
    def down_product(cut):
        return jnp.einsum("tf,td->fd", mixed_low, cut, preferred_element_type=jnp.float32)

    cot_mine, cot_theirs = halves(cotangent, 1)
    send_down = down_product(cot_theirs).astype(jnp.bfloat16)
    grad_mixed = jnp.einsum("td,fd->tf", cotangent, down_full, preferred_element_type=jnp.float32)
    (grad_lifted,) = geglu_back(grad_mixed)
    lifted_low = grad_lifted.astype(jnp.bfloat16)

    def in_product(cut):
        return jnp.einsum("td,tcf->dcf", cut, lifted_low, preferred_element_type=jnp.float32)

    hidden_mine, hidden_theirs = halves(hidden_two, 1)
    send_in = in_product(hidden_theirs).astype(jnp.bfloat16)
    hidden_two_part = jnp.einsum(
        "tcf,dcf->td", lifted_low, in_full, preferred_element_type=jnp.float32
    )
    grad_middle_norm, grad_mlp_gain = norm_two_back(core_sum(hidden_two_part))
    grad_middle = cotangent.astype(jnp.float32) + grad_middle_norm
    grad_branch = grad_middle.astype(jnp.bfloat16)

    def out_product(cut):
        return jnp.einsum("nt,td->nd", attn_low, cut, preferred_element_type=jnp.float32)

    branch_mine, branch_theirs = halves(grad_branch, 1)
    send_out = out_product(branch_theirs).astype(jnp.bfloat16)
    grad_attended = jnp.einsum(
        "td,nd->nt", grad_branch, out_full, preferred_element_type=jnp.float32
    ).astype(jnp.bfloat16)
    grad_attended, send_down, send_in, send_out = lax.optimization_barrier(
        (grad_attended, send_down, send_in, send_out)
    )
    down_arrived = swapped(send_down, "shard")
    in_arrived = swapped(send_in, "shard")
    out_arrived = swapped(send_out, "shard")
    own_grads = exchanged(grad_attended.reshape(ctx_size, own_heads, HD, tok_rows))
    own_packed = attention_backward(ends, packed, own_grads, own_attended, lse)
    own_packed, down_arrived, in_arrived, out_arrived = lax.optimization_barrier(
        (own_packed, down_arrived, in_arrived, out_arrived)
    )
    part_down = added(down_product(cot_mine), down_arrived)
    part_in = added(in_product(hidden_mine), in_arrived)
    part_out = added(out_product(branch_mine), out_arrived)
    own_packed, part_down, part_in, part_out = lax.optimization_barrier(
        (own_packed, part_down, part_in, part_out)
    )
    summed_early = lax.psum((part_in, part_down, part_out), "ctx")
    grad_packed = exchanged(own_packed).reshape(head_count, 3, HD, tok_rows)
    grad_projected = jnp.stack(
        [
            rotate_t(grad_packed[:, 0].astype(jnp.float32), cos_t, -sin_t).astype(jnp.bfloat16),
            rotate_t(grad_packed[:, 1].astype(jnp.float32), cos_t, -sin_t).astype(jnp.bfloat16),
            grad_packed[:, 2],
        ],
        axis=0,
    ).reshape(3, local_width, tok_rows)

    def qkv_product(cut):
        return jnp.einsum("td,cnt->dcn", cut, grad_projected, preferred_element_type=jnp.float32)

    one_mine, one_theirs = halves(hidden_one, 1)
    qkv_arrived = swapped(qkv_product(one_theirs).astype(jnp.bfloat16), "shard")
    hidden_one_part = jnp.einsum(
        "cnt,dcn->td", grad_projected, qkv_full, preferred_element_type=jnp.float32
    )
    grad_input_norm, grad_attn_gain = norm_one_back(core_sum(hidden_one_part))
    grad_tokens = (grad_middle + grad_input_norm).astype(jnp.bfloat16)
    gains_mine, gains_theirs = halves(jnp.stack([grad_attn_gain, grad_mlp_gain]), 1)
    gains = added(gains_mine, swapped(gains_theirs.astype(jnp.bfloat16), "shard"))
    part_qkv = added(qkv_product(one_mine), qkv_arrived)
    own_rows = part_qkv.shape[0]
    wide = part_qkv.reshape(ctx_size, own_rows // ctx_size, -1)
    extra = gains.reshape(ctx_size, 1, -1)
    extra = jnp.pad(extra, ((0, 0), (0, 15), (0, wide.shape[2] - extra.shape[2])))
    summed = block_sum(jnp.concatenate([wide, extra], axis=1))
    summed_qkv = summed[:, : wide.shape[1]].reshape(part_qkv.shape)
    gains = summed[:, wide.shape[1], : gains.size // ctx_size].reshape(gains.shape)
    return (
        output,
        grad_tokens,
        gains[0].astype(jnp.float32),
        summed_qkv.astype(jnp.float32),
        summed_early[2].astype(jnp.float32),
        gains[1].astype(jnp.float32),
        summed_early[0].astype(jnp.float32),
        summed_early[1].astype(jnp.float32),
    )


def layer(tokens, cotangent, lengths, g_attn, w_qkv, w_attn_out, g_mlp, w_in, w_mlp_out):
    head_count = w_qkv.shape[2] // HD
    whole_heads = head_count % lax.axis_size("ctx") == 0
    whole_heads = whole_heads and lax.axis_size("shard") == 2 and lax.axis_size("tp") == 2
    return (head_shards if whole_heads else shards)(
        tokens, cotangent, lengths, g_attn, w_qkv, w_attn_out, g_mlp, w_in, w_mlp_out
    )


def solution(mesh):
    return jax.shard_map(
        layer,
        mesh=mesh,
        in_specs=(
            P(("shard", "ctx"), None),
            P(("shard", "ctx"), None),
            P("shard", None),
            P("shard"),
            P("shard", None, "tp"),
            P("tp", "shard"),
            P("shard"),
            P("shard", None, "tp"),
            P("tp", "shard"),
        ),
        out_specs=(
            P(("shard", "ctx"), None),
            P(("shard", "ctx"), None),
            P("shard"),
            P("shard", None, "tp"),
            P("tp", "shard"),
            P("shard"),
            P("shard", None, "tp"),
            P("tp", "shard"),
        ),
        check_vma=False,
    )
```
